32 devices in a mesh: groups: 2 (over x), tok: 16 (over z, y, core).
Axes of the slice: x: 2, y: 2, z: 4, core: 2. Of those that a mesh axis runs over, the one named last changes fastest.
Arguments:
- queries: bfloat16 [4096, 4096], P(('groups', 'tok')), parts along dimension 0, may hold values from -8 to 8
- new_keys: bfloat16 [4096, 512], P(('groups', 'tok')), parts along dimension 0, may hold values from -8 to 8
- new_values: bfloat16 [4096, 512], P(('groups', 'tok')), parts along dimension 0, may hold values from -6 to 6
- cache_keys: bfloat16 [65536, 512], P(('groups', 'tok')), parts along dimension 0, may hold values from -8 to 8
- cache_values: bfloat16 [65536, 512], P(('groups', 'tok')), parts along dimension 0, may hold values from -6 to 6
- cache_lens: int32 [32], P(('groups', 'tok')), parts along dimension 0, may hold values from 1 to 2048, 20480 in all
- residual: bfloat16 [4096, 2048], P(('groups', 'tok')), parts along dimension 0, may hold values from -40 to 40
- out_weight: bfloat16 [4096, 2048], P('tok'), may hold values from -0.09375 to 0.09375
- norm_gain: float32 [2048], replicated, may hold values from 0.25 to 1.75
- expert_ids: int32 [4096, 8], P(('groups', 'tok')), parts along dimension 0, may hold values from 0 to 63, all different within a row; in each aligned block of 64 rows (0 to 63, 64 to 127, ...) at most 12 rows name the same one
- route_weights: float32 [4096, 8], P(('groups', 'tok')), parts along dimension 0, may hold values from 0.2 to 1
- gate_weight: bfloat16 [64, 2048, 384], P('tok'), may hold values from -0.125 to 0.125
- up_weight: bfloat16 [64, 2048, 384], P('tok'), may hold values from -0.125 to 0.125
- down_weight: bfloat16 [64, 384, 2048], P('tok'), may hold values from -0.3125 to 0.3125
Outputs:
- layer_out: bfloat16 [4096, 2048], P(('groups', 'tok')), parts along dimension 0
The draws below stay inside these ranges and needn't reach their ends.
There are 2 independent parts, one for each index of `groups`. The reference program is written for one: setup_inputs(seed, part) draws one part's arguments, and reference() takes and returns one part's arrays. A program takes and returns all parts, laid end to end along the dimension named above; an argument that names none is the same for every part. Nothing has to cross between parts.
Inputs may be any that keep to these rules, and one draw needn't show every extreme that they name: `expert_ids`: each row names 8 different experts. In each aligned block of 64 rows no expert is named by more than 12 rows; that many is reached in some block. `cache_lens`: the largest length equals 2048.
All inputs are finite; a program needn't handle non-finite values. No bound on the sum of `cache_lens` on one device may be relied on, other than what follows from the above.
Results may differ from the reference program's by a relative error of at most 0.009.
Values may be sent and summed in bfloat16 or wider, within the bound.
A program may use at most 128 MiB of HBM per device.

```python
import math
import jax
import jax.numpy as jnp
import numpy as np
from jax import lax

D = 2048
HEADS = 32
KVH = 4
HD = 128
FF = 384
TOPK = 8
ROWS = 128
CACHE = 2048
EXPERTS = 64
REQUESTS = 16
TOKENS = 2048
BLOCK = 64
CAP = 12


def draw_queries(key, part):
    first = jax.random.fold_in(key, 11)
    values = jnp.clip(jax.random.normal(first, (REQUESTS * ROWS, HEADS * HD), jnp.float32), -6.0, 6.0)
    return values.astype(jnp.bfloat16)


def draw_cache_keys(key, part):
    first = jax.random.fold_in(key, 23)
    values = jnp.clip(jax.random.normal(first, (REQUESTS * CACHE, KVH * HD), jnp.float32), -6.0, 6.0)
    return values.astype(jnp.bfloat16)


def draw_new_keys(key, part):
    first = jax.random.fold_in(key, 37)
    values = jnp.clip(jax.random.normal(first, (REQUESTS * ROWS, KVH * HD), jnp.float32), -6.0, 6.0)
    return values.astype(jnp.bfloat16)


def draw_residual(key, part):
    first = jax.random.fold_in(key, 53)
    values = jnp.clip(jax.random.normal(first, (REQUESTS * ROWS, D), jnp.float32), -6.0, 6.0)
    return values.astype(jnp.bfloat16)


def levels(rng, shape, shards, low, top_value):
    def one(axis_at, shards_of):
        steps = jax.random.uniform(jax.random.fold_in(jax.random.fold_in(rng, 6), axis_at), (shards_of,), jnp.float32, low / len(shards), top_value / len(shards))
        return jnp.repeat(jnp.exp(steps), shape[axis_at] // shards_of).reshape((-1,) + (1,) * (len(shape) - axis_at - 1))

    gain = one(*shards[0])
    for cut in shards[1:]:
        gain = gain * one(*cut)
    return gain


def length_profile(count, total, bound, skew):
    portions = [(1 << 20) // math.isqrt(grade ** skew) + 1 for grade in range(2, count + 1)]
    surplus, holding = total - bound - (count - 1), [1] * (count - 1)
    while surplus > 0:
        candidates = [i for i in range(count - 1) if holding[i] < bound]
        mass, budget = sum([portions[i] for i in candidates]), surplus
        for i in candidates:
            addition = min(bound - holding[i], max(1, budget * portions[i] // mass), surplus)
            holding[i] = holding[i] + addition
            surplus = surplus - addition
    return np.array([bound] + holding)


def ragged_sizes(key, amount, total, most, lean):
    if amount == 2:
        one = jax.random.randint(key, (), max(1, total - most), min(most, total - 1) + 1)
        return jnp.stack([one, total - one])
    lengths = jnp.asarray(length_profile(amount, total, most, lean), jnp.int32)
    couples = (amount - 1) // 2
    source_of, receiver = lengths[1:1 + 2 * couples:2], lengths[2:2 + 2 * couples:2]
    slack = jnp.minimum(source_of - 1, most - receiver)
    moved = jax.random.randint(jax.random.fold_in(key, 1), (couples,), 0, 1 << 20) % (slack + 1)
    lengths = lengths.at[1:1 + 2 * couples:2].set(source_of - moved).at[2:2 + 2 * couples:2].set(receiver + moved)
    return lengths[jax.random.permutation(jax.random.fold_in(key, 2), amount)]


def assign_block(key, own, number, rows, number_of, top, most, skew):
    order = jax.random.permutation(key, number_of)
    packed, ordinary = load_shares(number_of, rows * top, most, skew, True), load_shares(number_of, rows * top, most, skew, False)
    places = jnp.arange(number_of)

    def named(tallies, offset_by):
        used = int((tallies > 0).sum())
        fixed = max(1, used // 4)
        moved = fixed + (places - fixed + offset_by * (used - fixed)) % max(1, number_of - fixed)
        return jnp.zeros((number_of,), jnp.int32).at[order[jnp.where(places < fixed, places, moved)]].set(jnp.asarray(tallies, jnp.int32))

    tallies = jnp.where(number % 4 == 0, named(packed, number // 4), named(ordinary, number - number // 4 - 1))
    mixed = jax.random.permutation(jax.random.fold_in(own, 3), number_of)
    giver, taker = mixed[0:number_of // 2 * 2:2], mixed[1:number_of // 2 * 2:2]
    margin = jnp.minimum(tallies[giver] - 1, most - tallies[taker]) // 2
    margin = jnp.where((giver == order[0]) | (taker == order[0]) | (tallies[taker] == 0), 0, jnp.maximum(margin, 0))
    moved = jax.random.randint(jax.random.fold_in(own, 4), (number_of // 2,), 0, 1 << 20) % (margin + 1)
    tallies = tallies.at[giver].add(-moved).at[taker].add(moved)
    items = jnp.searchsorted(jnp.cumsum(tallies), jnp.arange(rows * top), side="right").astype(jnp.int32)
    table = items.reshape(top, rows).T
    table = table[jax.random.permutation(jax.random.fold_in(own, 1), rows)]
    offset_by = jax.random.randint(jax.random.fold_in(own, 2), (rows, 1), 0, top)
    return jnp.take_along_axis(table, (jnp.arange(top)[None, :] + offset_by) % top, axis=1)


def load_shares(count, total, limit, lean, full):
    weights = [(1 << 20) // math.isqrt(rank ** lean) + 1 for rank in range(1, count + 1)]
    largest = limit if full else min(limit, max(-(-total // count), total * weights[0] // sum(weights)))
    least = 1 if total - largest >= count - 1 else 0
    holding, rest = [largest] + [least] * (count - 1), total - largest - least * (count - 1)
    while rest > 0:
        free = [i for i in range(1, count) if holding[i] < largest] or [i for i in range(1, count) if holding[i] < limit]
        pool, budget = sum([weights[i] for i in free]), rest
        for i in free:
            addition = min(limit - holding[i], max(1, budget * weights[i] // pool), rest)
            holding[i] = holding[i] + addition
            rest = rest - addition
    return np.array(holding)


def normal_values(rng, extent, deviation, most, split=(), held_as=jnp.bfloat16):
    entries = deviation * jax.random.normal(rng, extent, jnp.float32)
    if split:
        entries = entries * levels(rng, extent, split, -0.22, 0.18)
    return jnp.clip(entries, -most, most).astype(held_as)


def setup_inputs(seed: int = 0, part: int = 0) -> dict:
    splits = jax.random.split(jax.random.key(seed), 15)
    part_splits = jax.random.split(jax.random.fold_in(splits[14], part), 15)
    queries = draw_queries(jax.random.fold_in(jax.random.fold_in(splits[14], part), 71), part)
    new_keys = draw_new_keys(jax.random.fold_in(jax.random.fold_in(splits[14], part), 71), part)
    new_values = normal_values(part_splits[2], (TOKENS, KVH * HD), 1.0, 6.0, ((0, 16),))
    cache_keys = draw_cache_keys(jax.random.fold_in(jax.random.fold_in(splits[14], part), 71), part)
    cache_values = normal_values(part_splits[4], (REQUESTS * CACHE, KVH * HD), 1.0, 6.0, ((0, 16),))
    cache_lens = ragged_sizes(part_splits[5], REQUESTS, REQUESTS * CACHE * 5 // 8, CACHE, 2).astype(jnp.int32)
    residual = draw_residual(jax.random.fold_in(jax.random.fold_in(splits[14], part), 71), part)
    out_weight = normal_values(splits[7], (HEADS * HD, D), (HEADS * HD) ** -0.5, 0.09375, ((0, 16),))
    norm_gain = jnp.clip(1.0 + 0.15 * jax.random.normal(splits[8], (D,), jnp.float32), 0.25, 1.75)
    expert_ids_keys = jax.random.split(jax.random.fold_in(part_splits[9], 1), TOKENS // BLOCK)
    expert_ids_turns = jax.random.permutation(jax.random.fold_in(part_splits[9], 3), TOKENS // BLOCK)
    expert_ids = jax.vmap(lambda own, number: assign_block(jax.random.fold_in(part_splits[9], 2), own, number, BLOCK, EXPERTS, TOPK, CAP, 2))(expert_ids_keys, expert_ids_turns).reshape((TOKENS, TOPK))
    route_weights = jnp.clip(0.2 + 0.8 * jax.random.uniform(part_splits[10], (TOKENS, TOPK), jnp.float32) ** levels(part_splits[10], (TOKENS, TOPK), ((0, 16),), -0.2, 0.2), 0.2, 1.0)
    gate_weight = normal_values(splits[11], (EXPERTS, D, FF), D ** -0.5, 0.125, ((0, 16),))
    up_weight = normal_values(splits[12], (EXPERTS, D, FF), D ** -0.5, 0.125, ((0, 16),))
    down_weight = normal_values(splits[13], (EXPERTS, FF, D), FF ** -0.5, 0.3125, ((0, 16),))
    return dict(queries=queries, new_keys=new_keys, new_values=new_values, cache_keys=cache_keys, cache_values=cache_values, cache_lens=cache_lens, residual=residual, out_weight=out_weight, norm_gain=norm_gain, expert_ids=expert_ids, route_weights=route_weights, gate_weight=gate_weight, up_weight=up_weight, down_weight=down_weight)


def reference(queries, new_keys, new_values, cache_keys, cache_values, cache_lens, residual, out_weight, norm_gain, expert_ids, route_weights, gate_weight, up_weight, down_weight):
    group = HEADS // KVH
    scale = HD ** (-0.5)

    def one_request(operands):
        query_rows, key_new, value_new, key_cache, value_cache, length = operands
        key_all = jnp.concatenate([key_cache, key_new], 0).astype(jnp.float32).reshape(-1, KVH, HD)
        value_all = jnp.concatenate([value_cache, value_new], 0).astype(jnp.float32).reshape(-1, KVH, HD)
        shaped = query_rows.astype(jnp.float32).reshape(ROWS, KVH, group, HD)
        scores = jnp.einsum('rcgd,kcd->crgk', shaped, key_all) * scale
        cache_ok = jnp.arange(CACHE, dtype=jnp.int32)[None, :] < length
        cache_ok = jnp.broadcast_to(cache_ok, (ROWS, CACHE))
        new_ok = jnp.arange(ROWS, dtype=jnp.int32)[None, :] <= jnp.arange(ROWS, dtype=jnp.int32)[:, None]
        allowed = jnp.concatenate([cache_ok, new_ok], 1)
        scores = jnp.where(allowed[None, :, None, :], scores, -1e+30)
        weights = jax.nn.softmax(scores, axis=-1).astype(jnp.bfloat16)
        output = jnp.einsum('crgk,kcd->rcgd', weights.astype(jnp.float32), value_all).astype(jnp.bfloat16)
        return output.reshape(ROWS, HEADS * HD)
    attended = lax.map(one_request, (queries.reshape(REQUESTS, ROWS, -1), new_keys.reshape(REQUESTS, ROWS, -1), new_values.reshape(REQUESTS, ROWS, -1), cache_keys.reshape(REQUESTS, CACHE, -1), cache_values.reshape(REQUESTS, CACHE, -1), cache_lens))
    attended = attended.reshape(REQUESTS * ROWS, HEADS * HD)
    mixed = residual.astype(jnp.float32) + jnp.dot(attended, out_weight, preferred_element_type=jnp.float32)
    factor = lax.rsqrt(lax.optimization_barrier(jnp.mean(mixed * mixed, axis=-1, keepdims=True)) + 1e-06)
    normed = (mixed * factor * norm_gain).astype(jnp.bfloat16)
    blocks_all = REQUESTS * ROWS // BLOCK
    flat_ids = expert_ids.reshape(blocks_all, BLOCK * TOPK)
    matches = (flat_ids[:, :, None] == jnp.arange(EXPERTS, dtype=jnp.int32)[None, None, :]).astype(jnp.int32)
    ranking = lax.optimization_barrier(jnp.sum(jnp.cumsum(matches, axis=1) * matches, axis=-1)) - 1
    block_index = jnp.arange(blocks_all, dtype=jnp.int32)[:, None]
    slot_index = ((flat_ids * blocks_all + block_index) * CAP + ranking).reshape(-1).astype(jnp.int32)
    token_index = (block_index * BLOCK + jnp.arange(BLOCK * TOPK, dtype=jnp.int32)[None, :] // TOPK).reshape(-1).astype(jnp.int32)
    total_slots = EXPERTS * blocks_all * CAP
    source_row = jnp.zeros((total_slots,), jnp.int32).at[slot_index].set(token_index)
    filled = jnp.zeros((total_slots,), jnp.bool_).at[slot_index].set(True)

    def one_expert(operands):
        rows_index, used, gate_matrix, up_matrix, down_matrix = operands
        gathered = jnp.where(used[:, None], normed[rows_index], jnp.zeros((), jnp.bfloat16))
        gate_part = jnp.dot(gathered, gate_matrix, preferred_element_type=jnp.float32)
        up_part = jnp.dot(gathered, up_matrix, preferred_element_type=jnp.float32)
        hidden = (jax.nn.silu(gate_part) * up_part).astype(jnp.bfloat16)
        return jnp.dot(hidden, down_matrix, preferred_element_type=jnp.float32).astype(jnp.bfloat16)
    results = lax.map(one_expert, (source_row.reshape(EXPERTS, -1), filled.reshape(EXPERTS, -1), gate_weight, up_weight, down_weight))
    picked = results.reshape(total_slots, D)[slot_index].astype(jnp.float32).reshape(-1, TOPK, D)
    combined = lax.optimization_barrier(jnp.sum(picked * route_weights[:, :, None], axis=1))
    return (mixed + combined).astype(jnp.bfloat16)
```

```python
import jax
import jax.numpy as jnp
from jax import lax
from jax.sharding import PartitionSpec as P

HEADS = 32
KVH = 4
HD = 128


def head_attention(query_rows, key_rows, value_rows, allowed):

    def one_head(operands):
        query_head, key_head, value_head = operands
        scores = jnp.einsum("rgd,kd->rgk", query_head, key_head, preferred_element_type=jnp.float32)
        scores = scores * query_head.shape[-1] ** (-0.5)
        scores = jnp.where(allowed[:, None, :], scores, -1e30)
        highest = jnp.max(scores, axis=-1, keepdims=True)
        weights = jnp.exp(scores - highest)
        weights = (weights / jnp.sum(weights, axis=-1, keepdims=True)).astype(jnp.bfloat16)
        return jnp.einsum(
            "rgk,kd->rgd", weights, value_head, preferred_element_type=jnp.float32
        ).astype(jnp.bfloat16)

    return lax.map(one_head, (query_rows, key_rows, value_rows))


def body(
    queries,
    new_keys,
    new_values,
    cache_keys,
    cache_values,
    cache_lens,
    residual,
    out_weight,
    norm_gain,
    expert_ids,
    route_weights,
    gate_weight,
    up_weight,
    down_weight,
):
    devices = lax.axis_size("tok")
    group = HEADS // KVH
    row_count = residual.shape[0]
    block_rows = row_count // 2
    top_count = expert_ids.shape[1]
    experts_local = gate_weight.shape[0]
    experts_all = experts_local * devices
    capacity = max(2, block_rows * top_count * 3 // (2 * experts_all))
    cache_rows = cache_keys.shape[0]
    length = cache_lens[0]
    key_all = jnp.concatenate([cache_keys, new_keys], 0).reshape(-1, KVH, HD).transpose(1, 0, 2)
    value_all = (
        jnp.concatenate([cache_values, new_values], 0).reshape(-1, KVH, HD).transpose(1, 0, 2)
    )
    place = lax.axis_index("tok")
    core = place % 2
    same_core = [list(range(parity, devices, 2)) for parity in range(2)]
    swap = [(i, i ^ 1) for i in range(devices)]
    core_weight = lax.all_gather(
        out_weight, "tok", axis=0, tiled=True, axis_index_groups=same_core
    )
    ids_all = lax.all_gather(expert_ids, "tok", axis=0)
    routes_all = lax.all_gather(route_weights, "tok", axis=0)
    positions = jnp.arange(row_count)
    cache_ok = jnp.broadcast_to(jnp.arange(cache_rows)[None, :] < length, (row_count, cache_rows))
    new_ok = jnp.arange(new_keys.shape[0])[None, :] <= positions[:, None]
    allowed = jnp.concatenate([cache_ok, new_ok], 1)
    shaped = queries.reshape(row_count, KVH, group, HD).transpose(1, 0, 2, 3)
    output = head_attention(shaped, key_all, value_all, allowed)
    attended = output.transpose(1, 0, 2, 3).reshape(row_count, devices // 2, 2, -1)
    own_columns = lax.dynamic_index_in_dim(attended, core, 2, keepdims=False)
    other_columns = lax.dynamic_index_in_dim(attended, 1 - core, 2, keepdims=False)
    own_columns = own_columns.reshape(row_count, -1)
    other_columns = other_columns.reshape(row_count, -1)
    sibling_rows = lax.ppermute(other_columns, "tok", swap)
    for_sibling = jnp.dot(
        sibling_rows, core_weight, preferred_element_type=jnp.float32
    ).astype(jnp.bfloat16)
    from_sibling = lax.ppermute(for_sibling, "tok", swap)
    own_part = jnp.dot(own_columns, core_weight, preferred_element_type=jnp.float32)
    mixed = residual.astype(jnp.float32) + own_part + from_sibling.astype(jnp.float32)
    factor = lax.rsqrt(jnp.mean(mixed * mixed, axis=-1, keepdims=True) + 1e-06)
    normed = (mixed * factor * norm_gain).astype(jnp.bfloat16)
    own_experts = place * experts_local + jnp.arange(experts_local)
    earlier = (jnp.arange(block_rows)[:, None] > jnp.arange(block_rows)[None, :]).astype(
        jnp.bfloat16
    )
    pieces = []
    for half in range(2):
        lower = half * block_rows
        upper = lower + block_rows
        gathered = lax.all_gather(normed[lower:upper], "tok", axis=0, tiled=True)
        hits = ids_all[:, lower:upper, :, None] == own_experts
        chosen = jnp.any(hits, axis=2)
        weight = jnp.sum(
            jnp.where(hits, routes_all[:, lower:upper, :, None], 0.0), axis=2
        )
        rank = jnp.einsum(
            "ij,bje->bie", earlier, chosen.astype(jnp.bfloat16), preferred_element_type=jnp.float32
        ).astype(jnp.int32)
        rank = jnp.where(chosen, rank, -1)
        pick = rank[:, :, :, None] == jnp.arange(capacity)
        weight_slot = jnp.sum(jnp.where(pick, weight[..., None], 0.0), axis=1)
        weight_slot = weight_slot.transpose(1, 0, 2).reshape(experts_local, devices * capacity, 1)
        same = jnp.arange(devices)[:, None] == jnp.arange(devices)[None, :]
        spread = pick[:, :, :, None, :] & same[:, None, None, :, None]
        spread = spread.transpose(2, 3, 4, 0, 1).reshape(
            experts_local * devices * capacity, devices * block_rows
        ).astype(jnp.bfloat16)
        stacked = jnp.dot(spread, gathered, preferred_element_type=jnp.bfloat16)
        stacked = stacked.reshape(experts_local, devices * capacity, -1)
        gate_part = jnp.einsum(
            "erd,edf->erf", stacked, gate_weight, preferred_element_type=jnp.float32
        )
        up_part = jnp.einsum("erd,edf->erf", stacked, up_weight, preferred_element_type=jnp.float32)
        hidden = (jax.nn.silu(gate_part) * up_part).astype(jnp.bfloat16)
        result = jnp.einsum("erf,efd->erd", hidden, down_weight, preferred_element_type=jnp.float32)
        result = (result * weight_slot).astype(jnp.bfloat16)
        result = result.reshape(experts_local * devices * capacity, -1)
        summed = jnp.einsum(
            "sr,sd->rd", spread, result, preferred_element_type=jnp.float32
        ).astype(jnp.bfloat16)
        share = lax.psum_scatter(summed, "tok", scatter_dimension=0, tiled=True)
        pieces.append(mixed[lower:upper] + share.astype(jnp.float32))
    final = jnp.concatenate(pieces, 0)
    return final.astype(jnp.bfloat16)


def solution(mesh):
    placed = (
        P(("groups", "tok"), None),
        P(("groups", "tok"), None),
        P(("groups", "tok"), None),
        P(("groups", "tok"), None),
        P(("groups", "tok"), None),
        P(("groups", "tok")),
        P(("groups", "tok"), None),
        P("tok", None),
        P(),
        P(("groups", "tok"), None),
        P(("groups", "tok"), None),
        P("tok", None, None),
        P("tok", None, None),
        P("tok", None, None),
    )
    return jax.shard_map(
        body, mesh=mesh, in_specs=placed, out_specs=P(("groups", "tok"), None), check_vma=False
    )
```

```python
import jax
import jax.numpy as jnp
import functools

from jax import lax
from jax.experimental import pallas as pl
from jax.experimental.pallas import tpu as pltpu
from jax.sharding import PartitionSpec as P

MESH = pl.DeviceIdType.MESH

HEADS = 32
KVH = 4
HD = 128


def head_attention(query_rows, key_rows, value_rows, allowed):

    def one_head(operands):
        query_head, key_head, value_head = operands
        scores = jnp.einsum("rgd,kd->rgk", query_head, key_head, preferred_element_type=jnp.float32)
        scores = scores * query_head.shape[-1] ** (-0.5)
        scores = jnp.where(allowed[:, None, :], scores, -1e30)
        highest = jnp.max(scores, axis=-1, keepdims=True)
        weights = jnp.exp(scores - highest)
        weights = (weights / jnp.sum(weights, axis=-1, keepdims=True)).astype(jnp.bfloat16)
        return jnp.einsum(
            "rgk,kd->rgd", weights, value_head, preferred_element_type=jnp.float32
        ).astype(jnp.bfloat16)

    return lax.map(one_head, (query_rows, key_rows, value_rows))


def place_of(count):
    place = lax.axis_index("tok")
    return place // 4, (place // 2) % 2, place % 2, count // 4


def greet(level, row, core, levels):
    barrier = pltpu.get_barrier_semaphore()

    def tell(level_to, row_to, core_to):
        pl.semaphore_signal(
            barrier,
            inc=1,
            device_id={"tok": (level_to * 2 + row_to) * 2 + core_to},
            device_id_type=MESH,
        )

    tell(level, 1 - row, core)
    tell(level, row, 1 - core)

    @pl.when(level > 0)
    def _():
        tell(level - 1, row, core)

    @pl.when(level < levels - 1)
    def _():
        tell(level + 1, row, core)

    ends = (level > 0).astype(jnp.int32) + (level < levels - 1).astype(jnp.int32)
    pl.semaphore_wait(barrier, 2 + ends)


def gather_kernel(count, rows_ref, aux_ref, all_rows, all_aux, own_sem, send_sem, recv_sem):
    level, row, core, levels = place_of(count)
    greet(level, row, core, levels)
    me = lax.axis_index("tok")

    def sends(block, way, target, first):
        out = []
        pairs = ((rows_ref, all_rows), (aux_ref, all_aux))
        for which, (own, everyone) in enumerate(pairs):
            out.append(
                pltpu.make_async_remote_copy(
                    src_ref=own if first else everyone.at[block],
                    dst_ref=everyone.at[block],
                    send_sem=send_sem.at[which, way, block],
                    recv_sem=recv_sem.at[which, block],
                    device_id={"tok": target},
                    device_id_type=MESH,
                )
            )
        return out

    def each(block, act, first=False, up=None, down=None, across=True):
        if up is not None:
            @pl.when(up)
            def _():
                for copy in sends(block, 0, me + 4, first):
                    act(copy)
        if down is not None:
            @pl.when(down)
            def _():
                for copy in sends(block, 1, me - 4, first):
                    act(copy)
        if across:
            for copy in sends(block, 2, (level * 2 + 1 - row) * 2 + core, first):
                act(copy)
        for copy in sends(block, 3, (level * 2 + row) * 2 + 1 - core, first):
            act(copy)

    def arrived(block):
        for copy in sends(block, 3, (level * 2 + row) * 2 + 1 - core, False):
            copy.wait_recv()

    start = lambda copy: copy.start()
    done = lambda copy: copy.wait_send()
    can_up, can_down = level < levels - 1, level > 0

    def line_step(distance, act, receive):
        @pl.when(level >= distance)
        def _():
            block = me - 4 * distance
            if receive:
                arrived(block)
            each(block, act, up=can_up)

        @pl.when(level + distance < levels)
        def _():
            block = me + 4 * distance
            if receive:
                arrived(block)
            each(block, act, down=can_down)

    def row_step(distance, act, receive):
        def one(level_from):
            block = (level_from * 2 + 1 - row) * 2 + core
            if receive:
                arrived(block)
            each(block, act, across=False)

        if distance == 0:
            one(level)
        else:
            @pl.when(level >= distance)
            def _():
                one(level - distance)

            @pl.when(level + distance < levels)
            def _():
                one(level + distance)

    each(me, start, first=True, up=can_up, down=can_down)
    own_rows = pltpu.make_async_copy(rows_ref, all_rows.at[me], own_sem.at[0])
    own_aux = pltpu.make_async_copy(aux_ref, all_aux.at[me], own_sem.at[1])
    own_rows.start()
    own_aux.start()
    for step in range(1, levels + 1):
        if step < levels:
            line_step(step, start, True)
        row_step(step - 1, start, True)
    for index in range(count // 2):
        arrived(index * 2 + 1 - core)
    each(me, done, first=True, up=can_up, down=can_down)
    for step in range(1, levels):
        line_step(step, done, False)
    for step in range(levels):
        row_step(step, done, False)
    own_rows.wait()
    own_aux.wait()


def gather_rows(rows, aux, count):
    anywhere = pl.BlockSpec(memory_space=pl.ANY)
    return pl.pallas_call(
        functools.partial(gather_kernel, count),
        out_shape=(
            jax.ShapeDtypeStruct((count,) + rows.shape, rows.dtype),
            jax.ShapeDtypeStruct((count,) + aux.shape, aux.dtype),
        ),
        in_specs=[anywhere, anywhere],
        out_specs=(anywhere, anywhere),
        scratch_shapes=[
            pltpu.SemaphoreType.DMA((2,)),
            pltpu.SemaphoreType.DMA((2, 4, count)),
            pltpu.SemaphoreType.DMA((2, count)),
        ],
        compiler_params=pltpu.CompilerParams(collective_id=0, has_side_effects=True),
    )(rows, aux)


def sum_kernel(
    count, parts, mixed, out, from_core, from_row, total, from_below, from_above,
    core_sem, row_sem, up_sem, down_sem,
):
    level, row, core, levels = place_of(count)
    greet(level, row, core, levels)
    me = lax.axis_index("tok")
    row_count = mixed.shape[0]
    tile = 16

    def tiles(act):
        @pl.loop(0, row_count // tile)
        def _(index):
            act(pl.ds(pl.multiple_of(index * tile, tile), tile))

    def remote(src, dst, sems, index, target):
        return pltpu.make_async_remote_copy(
            src_ref=src,
            dst_ref=dst,
            send_sem=sems.at[0, index],
            recv_sem=sems.at[1, index],
            device_id={"tok": target},
            device_id_type=MESH,
        )

    def to_core(level_to, row_to):
        slot = level_to * 2 + row_to
        target = (level * 2 + row) * 2 + 1 - core
        return remote(parts.at[slot * 2 + 1 - core], from_core.at[slot], core_sem, slot, target)

    def to_row(level_to):
        target = (level * 2 + 1 - row) * 2 + core
        slot = level_to * 2 + 1 - row
        return remote(from_core.at[slot], from_row.at[level_to], row_sem, level_to, target)

    def to_up(level_to):
        return remote(total.at[level_to], from_below.at[level_to], up_sem, level_to, me + 4)

    def to_down(level_to):
        return remote(total.at[level_to], from_above.at[level_to], down_sem, level_to, me - 4)

    def in_order(act):
        for step in range(levels - 1):
            high, low = levels - 1 - step, step

            @pl.when(high > level)
            def _():
                act(high, 1)

            @pl.when(low < level)
            def _():
                act(low, -1)

        act(level, 0)

    for row_to in (1 - row, row):
        in_order(lambda level_to, way, row_to=row_to: to_core(level_to, row_to).start())

    def pass_row(level_to, way):
        slot = level_to * 2 + 1 - row
        to_core(level_to, 1 - row).wait_recv()

        def add(where):
            both = parts[slot * 2 + core, where, :].astype(jnp.float32) + from_core[
                slot, where, :
            ].astype(jnp.float32)
            from_core[slot, where, :] = both.astype(jnp.bfloat16)

        tiles(add)
        to_row(level_to).start()

    in_order(pass_row)

    def base(slot, level_to, where):
        return (
            parts[slot * 2 + core, where, :].astype(jnp.float32)
            + from_core[slot, where, :].astype(jnp.float32)
            + from_row[level_to, where, :].astype(jnp.float32)
        )

    def pass_line(level_to, way):
        slot = level_to * 2 + row
        to_core(level_to, row).wait_recv()
        to_row(level_to).wait_recv()
        if way == 0:
            def keep(where):
                total[level_to, where, :] = base(slot, level_to, where).astype(jnp.bfloat16)

            def finish(where):
                out[where, :] = mixed[where, :] + base(slot, level_to, where)

            tiles(finish)
            for neighbour, incoming, copy in (
                (level > 0, from_below, to_up),
                (level < levels - 1, from_above, to_down),
            ):
                @pl.when(neighbour)
                def _(incoming=incoming, copy=copy):
                    copy(level_to).wait_recv()

                    def more(where):
                        out[where, :] += incoming[level_to, where, :].astype(jnp.float32)

                    tiles(more)
            return
        behind = level > 0 if way == 1 else level < levels - 1
        incoming, copy = (from_below, to_up) if way == 1 else (from_above, to_down)

        @pl.when(behind)
        def _():
            copy(level_to).wait_recv()

            def add(where):
                value = base(slot, level_to, where) + incoming[level_to, where, :].astype(
                    jnp.float32
                )
                total[level_to, where, :] = value.astype(jnp.bfloat16)

            tiles(add)

        @pl.when(jnp.logical_not(behind))
        def _():
            def add(where):
                total[level_to, where, :] = base(slot, level_to, where).astype(jnp.bfloat16)

            tiles(add)

        copy(level_to).start()

    in_order(pass_line)
    for row_to in (1 - row, row):
        in_order(lambda level_to, way, row_to=row_to: to_core(level_to, row_to).wait_send())
    in_order(lambda level_to, way: to_row(level_to).wait_send())

    def sent(level_to, way):
        if way == 1:
            to_up(level_to).wait_send()
        if way == -1:
            to_down(level_to).wait_send()

    in_order(sent)


def sum_rows(parts, mixed, count):
    row_count, width = mixed.shape
    levels = count // 4
    inside = pl.BlockSpec(memory_space=pltpu.VMEM)

    def blocks(number):
        return pltpu.VMEM((number, row_count, width), jnp.bfloat16)

    return pl.pallas_call(
        functools.partial(sum_kernel, count),
        out_shape=jax.ShapeDtypeStruct(mixed.shape, jnp.float32),
        in_specs=[inside, inside],
        out_specs=inside,
        scratch_shapes=[
            blocks(count // 2),
            blocks(levels),
            blocks(levels),
            blocks(levels),
            blocks(levels),
            pltpu.SemaphoreType.DMA((2, count // 2)),
            pltpu.SemaphoreType.DMA((2, levels)),
            pltpu.SemaphoreType.DMA((2, levels)),
            pltpu.SemaphoreType.DMA((2, levels)),
        ],
        compiler_params=pltpu.CompilerParams(
            collective_id=1, has_side_effects=True, vmem_limit_bytes=56 * 2**20
        ),
    )(parts, mixed)


def expert_kernel(
    capacity, slots, top_count, aux, rows, gate, up, down, out, picks, scale, stacked, results
):
    step = pl.program_id(0)
    experts_local = stacked.shape[0]
    groups = stacked.shape[1]
    row_count = aux.shape[2]
    block_rows = row_count // 2
    width = 2 * row_count

    @pl.when(step == 0)
    def _():
        first = (lax.axis_index("tok") * experts_local).astype(jnp.float32)
        before = lax.broadcasted_iota(jnp.int32, (width, width), 0)
        after = lax.broadcasted_iota(jnp.int32, (width, width), 1)
        earlier = ((before < after) & (before // block_rows == after // block_rows)).astype(
            jnp.bfloat16
        )
        block = (lax.broadcasted_iota(jnp.int32, (1, width), 1) // block_rows) * capacity
        slot = lax.broadcasted_iota(jnp.int32, (slots, width), 0).astype(jnp.float32)

        @pl.loop(0, groups)
        def _(group):
            both = jnp.concatenate([aux[group * 2], aux[group * 2 + 1]], axis=1)
            ids, routes = both[:top_count], both[top_count:]
            for expert in range(experts_local):
                hit = (ids == first + expert).astype(jnp.float32)
                chosen = jnp.sum(hit, axis=0, keepdims=True)
                weight = jnp.sum(hit * routes, axis=0, keepdims=True)
                rank = jnp.dot(
                    jnp.broadcast_to(chosen, (16, width)).astype(jnp.bfloat16),
                    earlier,
                    preferred_element_type=jnp.float32,
                )[:1]
                target = jnp.where(chosen > 0.5, rank + block.astype(jnp.float32), -1.0)
                pick = (slot == target).astype(jnp.float32)
                picks[group, expert * slots : (expert + 1) * slots, :] = pick.astype(jnp.bfloat16)
                scale[expert, group] = jnp.sum(pick * weight, axis=1, keepdims=True)
            source = rows[pl.ds(pl.multiple_of(group * width, width), width), :]
            taken = jnp.dot(picks[group], source, preferred_element_type=jnp.float32)
            taken = taken.astype(jnp.bfloat16)
            for expert in range(experts_local):
                stacked[expert, group] = taken[expert * slots : (expert + 1) * slots]

    depth = stacked.shape[-1]
    inputs = stacked[step].reshape(groups * slots, depth)
    gate_part = jnp.dot(inputs, gate[0], preferred_element_type=jnp.float32)
    up_part = jnp.dot(inputs, up[0], preferred_element_type=jnp.float32)
    hidden = (gate_part / (1.0 + jnp.exp(-gate_part)) * up_part).astype(jnp.bfloat16)
    result = jnp.dot(hidden, down[0], preferred_element_type=jnp.float32)
    result = result * scale[step].reshape(groups * slots, 1)
    results[step] = result.astype(jnp.bfloat16).reshape(groups, slots, depth)

    @pl.when(step == experts_local - 1)
    def _():
        @pl.loop(0, groups)
        def _(group):
            value = jnp.concatenate([results[e, group] for e in range(experts_local)], axis=0)
            summed = lax.dot_general(
                picks[group], value, (((0,), (0,)), ((), ())), preferred_element_type=jnp.float32
            )
            out[pl.ds(pl.multiple_of(group * width, width), width), :] = summed.astype(
                jnp.bfloat16
            )


def run_experts(aux, rows, gate_weight, up_weight, down_weight, capacity):
    count, doubled, row_count = aux.shape
    experts_local, depth, hidden = gate_weight.shape
    groups = count // 2
    slots = -(-4 * capacity // 16) * 16
    whole = dict(pipeline_mode=pl.Buffered(1))
    return pl.pallas_call(
        functools.partial(expert_kernel, capacity, slots, doubled // 2),
        grid=(experts_local,),
        out_shape=jax.ShapeDtypeStruct(rows.shape, jnp.bfloat16),
        in_specs=[
            pl.BlockSpec(aux.shape, lambda e: (0, 0, 0), **whole),
            pl.BlockSpec(rows.shape, lambda e: (0, 0), **whole),
            pl.BlockSpec((1, depth, hidden), lambda e: (e, 0, 0)),
            pl.BlockSpec((1, depth, hidden), lambda e: (e, 0, 0)),
            pl.BlockSpec((1, hidden, depth), lambda e: (e, 0, 0)),
        ],
        out_specs=pl.BlockSpec(rows.shape, lambda e: (0, 0), **whole),
        scratch_shapes=[
            pltpu.VMEM((groups, experts_local * slots, 2 * row_count), jnp.bfloat16),
            pltpu.VMEM((experts_local, groups, slots, 1), jnp.float32),
            pltpu.VMEM((experts_local, groups, slots, depth), jnp.bfloat16),
            pltpu.VMEM((experts_local, groups, slots, depth), jnp.bfloat16),
        ],
        compiler_params=pltpu.CompilerParams(
            dimension_semantics=("arbitrary",), vmem_limit_bytes=62 * 2**20
        ),
    )(aux, rows, gate_weight, up_weight, down_weight)


def body(
    queries,
    new_keys,
    new_values,
    cache_keys,
    cache_values,
    cache_lens,
    residual,
    out_weight,
    norm_gain,
    expert_ids,
    route_weights,
    gate_weight,
    up_weight,
    down_weight,
):
    devices = lax.axis_size("tok")
    group = HEADS // KVH
    row_count = residual.shape[0]
    block_rows = row_count // 2
    top_count = expert_ids.shape[1]
    experts_local = gate_weight.shape[0]
    experts_all = experts_local * devices
    capacity = max(2, block_rows * top_count * 3 // (2 * experts_all))
    cache_rows = cache_keys.shape[0]
    length = cache_lens[0]
    key_all = jnp.concatenate([cache_keys, new_keys], 0).reshape(-1, KVH, HD).transpose(1, 0, 2)
    value_all = (
        jnp.concatenate([cache_values, new_values], 0).reshape(-1, KVH, HD).transpose(1, 0, 2)
    )
    place = lax.axis_index("tok")
    core = place % 2
    same_core = [list(range(parity, devices, 2)) for parity in range(2)]
    swap = [(i, i ^ 1) for i in range(devices)]
    core_weight = lax.all_gather(
        out_weight, "tok", axis=0, tiled=True, axis_index_groups=same_core
    )
    positions = jnp.arange(row_count)
    cache_ok = jnp.broadcast_to(jnp.arange(cache_rows)[None, :] < length, (row_count, cache_rows))
    new_ok = jnp.arange(new_keys.shape[0])[None, :] <= positions[:, None]
    allowed = jnp.concatenate([cache_ok, new_ok], 1)
    shaped = queries.reshape(row_count, KVH, group, HD).transpose(1, 0, 2, 3)
    output = head_attention(shaped, key_all, value_all, allowed)
    attended = output.transpose(1, 0, 2, 3).reshape(row_count, devices // 2, 2, -1)
    own_columns = lax.dynamic_index_in_dim(attended, core, 2, keepdims=False)
    other_columns = lax.dynamic_index_in_dim(attended, 1 - core, 2, keepdims=False)
    own_columns = own_columns.reshape(row_count, -1)
    other_columns = other_columns.reshape(row_count, -1)
    sibling_rows = lax.ppermute(other_columns, "tok", swap)
    for_sibling = jnp.dot(
        sibling_rows, core_weight, preferred_element_type=jnp.float32
    ).astype(jnp.bfloat16)
    from_sibling = lax.ppermute(for_sibling, "tok", swap)
    own_part = jnp.dot(own_columns, core_weight, preferred_element_type=jnp.float32)
    mixed = residual.astype(jnp.float32) + own_part + from_sibling.astype(jnp.float32)
    factor = lax.rsqrt(jnp.mean(mixed * mixed, axis=-1, keepdims=True) + 1e-06)
    normed = (mixed * factor * norm_gain).astype(jnp.bfloat16)
    aux = jnp.concatenate([expert_ids.astype(jnp.float32).T, route_weights.T], axis=0)
    all_rows, all_aux = gather_rows(normed, aux, devices)
    summed = run_experts(
        all_aux,
        all_rows.reshape(devices * row_count, -1),
        gate_weight,
        up_weight,
        down_weight,
        capacity,
    )
    final = sum_rows(summed.reshape(devices, row_count, -1), mixed, devices)
    return final.astype(jnp.bfloat16)


def solution(mesh):
    placed = (
        P(("groups", "tok"), None),
        P(("groups", "tok"), None),
        P(("groups", "tok"), None),
        P(("groups", "tok"), None),
        P(("groups", "tok"), None),
        P(("groups", "tok")),
        P(("groups", "tok"), None),
        P("tok", None),
        P(),
        P(("groups", "tok"), None),
        P(("groups", "tok"), None),
        P("tok", None, None),
        P("tok", None, None),
        P("tok", None, None),
    )
    return jax.shard_map(
        body, mesh=mesh, in_specs=placed, out_specs=P(("groups", "tok"), None), check_vma=False
    )
```

```python
import jax
import jax.numpy as jnp
import functools

from jax import lax
from jax.experimental import pallas as pl
from jax.experimental.pallas import tpu as pltpu
from jax.sharding import PartitionSpec as P

MESH = pl.DeviceIdType.MESH

HEADS = 32
KVH = 4
HD = 128


def head_attention(query_rows, key_rows, value_rows, allowed):

    def one_head(operands):
        query_head, key_head, value_head = operands
        scores = jnp.einsum("rgd,kd->rgk", query_head, key_head, preferred_element_type=jnp.float32)
        scores = scores * query_head.shape[-1] ** (-0.5)
        scores = jnp.where(allowed[:, None, :], scores, -1e30)
        highest = jnp.max(scores, axis=-1, keepdims=True)
        weights = jnp.exp(scores - highest)
        weights = (weights / jnp.sum(weights, axis=-1, keepdims=True)).astype(jnp.bfloat16)
        return jnp.einsum(
            "rgk,kd->rgd", weights, value_head, preferred_element_type=jnp.float32
        ).astype(jnp.bfloat16)

    return lax.map(one_head, (query_rows, key_rows, value_rows))


def place_of(count):
    place = lax.axis_index("tok")
    return place // 4, (place // 2) % 2, place % 2, count // 4


def greet(level, row, core, levels):
    barrier = pltpu.get_barrier_semaphore()

    def tell(level_to, row_to, core_to):
        pl.semaphore_signal(
            barrier,
            inc=1,
            device_id={"tok": (level_to * 2 + row_to) * 2 + core_to},
            device_id_type=MESH,
        )

    tell(level, 1 - row, core)
    tell(level, row, 1 - core)

    @pl.when(level > 0)
    def _():
        tell(level - 1, row, core)

    @pl.when(level < levels - 1)
    def _():
        tell(level + 1, row, core)

    ends = (level > 0).astype(jnp.int32) + (level < levels - 1).astype(jnp.int32)
    pl.semaphore_wait(barrier, 2 + ends)


def gather_kernel(count, rows_ref, aux_ref, all_rows, all_aux, own_sem, send_sem, recv_sem):
    level, row, core, levels = place_of(count)
    greet(level, row, core, levels)
    me = lax.axis_index("tok")

    def sends(block, way, target, first):
        out = []
        pairs = ((rows_ref, all_rows), (aux_ref, all_aux))
        for which, (own, everyone) in enumerate(pairs):
            out.append(
                pltpu.make_async_remote_copy(
                    src_ref=own if first else everyone.at[block],
                    dst_ref=everyone.at[block],
                    send_sem=send_sem.at[which, way, block],
                    recv_sem=recv_sem.at[which, block],
                    device_id={"tok": target},
                    device_id_type=MESH,
                )
            )
        return out

    def each(block, act, first=False, up=None, down=None, across=True):
        if up is not None:
            @pl.when(up)
            def _():
                for copy in sends(block, 0, me + 4, first):
                    act(copy)
        if down is not None:
            @pl.when(down)
            def _():
                for copy in sends(block, 1, me - 4, first):
                    act(copy)
        if across:
            for copy in sends(block, 2, (level * 2 + 1 - row) * 2 + core, first):
                act(copy)
        for copy in sends(block, 3, (level * 2 + row) * 2 + 1 - core, first):
            act(copy)

    def arrived(block):
        for copy in sends(block, 3, (level * 2 + row) * 2 + 1 - core, False):
            copy.wait_recv()

    start = lambda copy: copy.start()
    done = lambda copy: copy.wait_send()
    can_up, can_down = level < levels - 1, level > 0

    def line_step(distance, act, receive):
        @pl.when(level >= distance)
        def _():
            block = me - 4 * distance
            if receive:
                arrived(block)
            each(block, act, up=can_up)

        @pl.when(level + distance < levels)
        def _():
            block = me + 4 * distance
            if receive:
                arrived(block)
            each(block, act, down=can_down)

    def row_step(distance, act, receive):
        def one(level_from):
            block = (level_from * 2 + 1 - row) * 2 + core
            if receive:
                arrived(block)
            each(block, act, across=False)

        if distance == 0:
            one(level)
        else:
            @pl.when(level >= distance)
            def _():
                one(level - distance)

            @pl.when(level + distance < levels)
            def _():
                one(level + distance)

    each(me, start, first=True, up=can_up, down=can_down)
    own_rows = pltpu.make_async_copy(rows_ref, all_rows.at[me], own_sem.at[0])
    own_aux = pltpu.make_async_copy(aux_ref, all_aux.at[me], own_sem.at[1])
    own_rows.start()
    own_aux.start()
    for step in range(1, levels + 1):
        if step < levels:
            line_step(step, start, True)
        row_step(step - 1, start, True)
    for index in range(count // 2):
        arrived(index * 2 + 1 - core)
    each(me, done, first=True, up=can_up, down=can_down)
    for step in range(1, levels):
        line_step(step, done, False)
    for step in range(levels):
        row_step(step, done, False)
    own_rows.wait()
    own_aux.wait()


def gather_rows(rows, aux, count):
    anywhere = pl.BlockSpec(memory_space=pl.ANY)
    return pl.pallas_call(
        functools.partial(gather_kernel, count),
        out_shape=(
            jax.ShapeDtypeStruct((count,) + rows.shape, rows.dtype),
            jax.ShapeDtypeStruct((count,) + aux.shape, aux.dtype),
        ),
        in_specs=[anywhere, anywhere],
        out_specs=(anywhere, anywhere),
        scratch_shapes=[
            pltpu.SemaphoreType.DMA((2,)),
            pltpu.SemaphoreType.DMA((2, 4, count)),
            pltpu.SemaphoreType.DMA((2, count)),
        ],
        compiler_params=pltpu.CompilerParams(collective_id=0, has_side_effects=True),
    )(rows, aux)


def sum_kernel(
    count, parts, mixed, out, from_core, from_row, total, from_below, from_above,
    core_sem, row_sem, up_sem, down_sem,
):
    level, row, core, levels = place_of(count)
    greet(level, row, core, levels)
    me = lax.axis_index("tok")
    row_count = mixed.shape[0]
    tile = 16

    def tiles(act):
        @pl.loop(0, row_count // tile)
        def _(index):
            act(pl.ds(pl.multiple_of(index * tile, tile), tile))

    def remote(src, dst, sems, index, target):
        return pltpu.make_async_remote_copy(
            src_ref=src,
            dst_ref=dst,
            send_sem=sems.at[0, index],
            recv_sem=sems.at[1, index],
            device_id={"tok": target},
            device_id_type=MESH,
        )

    def to_core(level_to, row_to):
        slot = level_to * 2 + row_to
        target = (level * 2 + row) * 2 + 1 - core
        return remote(parts.at[slot * 2 + 1 - core], from_core.at[slot], core_sem, slot, target)

    def to_row(level_to):
        target = (level * 2 + 1 - row) * 2 + core
        slot = level_to * 2 + 1 - row
        return remote(from_core.at[slot], from_row.at[level_to], row_sem, level_to, target)

    def to_up(level_to):
        return remote(total.at[level_to], from_below.at[level_to], up_sem, level_to, me + 4)

    def to_down(level_to):
        return remote(total.at[level_to], from_above.at[level_to], down_sem, level_to, me - 4)

    def in_order(act):
        for step in range(levels - 1):
            high, low = levels - 1 - step, step

            @pl.when(high > level)
            def _():
                act(high, 1)

            @pl.when(low < level)
            def _():
                act(low, -1)

        act(level, 0)

    for row_to in (1 - row, row):
        in_order(lambda level_to, way, row_to=row_to: to_core(level_to, row_to).start())

    def pass_row(level_to, way):
        slot = level_to * 2 + 1 - row
        to_core(level_to, 1 - row).wait_recv()

        def add(where):
            both = parts[slot * 2 + core, where, :].astype(jnp.float32) + from_core[
                slot, where, :
            ].astype(jnp.float32)
            from_core[slot, where, :] = both.astype(jnp.bfloat16)

        tiles(add)
        to_row(level_to).start()

    in_order(pass_row)

    def base(slot, level_to, where):
        return (
            parts[slot * 2 + core, where, :].astype(jnp.float32)
            + from_core[slot, where, :].astype(jnp.float32)
            + from_row[level_to, where, :].astype(jnp.float32)
        )

    def pass_line(level_to, way):
        slot = level_to * 2 + row
        to_core(level_to, row).wait_recv()
        to_row(level_to).wait_recv()
        if way == 0:
            def keep(where):
                total[level_to, where, :] = base(slot, level_to, where).astype(jnp.bfloat16)

            def finish(where):
                out[where, :] = mixed[where, :] + base(slot, level_to, where)

            tiles(finish)
            for neighbour, incoming, copy in (
                (level > 0, from_below, to_up),
                (level < levels - 1, from_above, to_down),
            ):
                @pl.when(neighbour)
                def _(incoming=incoming, copy=copy):
                    copy(level_to).wait_recv()

                    def more(where):
                        out[where, :] += incoming[level_to, where, :].astype(jnp.float32)

                    tiles(more)
            return
        behind = level > 0 if way == 1 else level < levels - 1
        incoming, copy = (from_below, to_up) if way == 1 else (from_above, to_down)

        @pl.when(behind)
        def _():
            copy(level_to).wait_recv()

            def add(where):
                value = base(slot, level_to, where) + incoming[level_to, where, :].astype(
                    jnp.float32
                )
                total[level_to, where, :] = value.astype(jnp.bfloat16)

            tiles(add)

        @pl.when(jnp.logical_not(behind))
        def _():
            def add(where):
                total[level_to, where, :] = base(slot, level_to, where).astype(jnp.bfloat16)

            tiles(add)

        copy(level_to).start()

    in_order(pass_line)
    for row_to in (1 - row, row):
        in_order(lambda level_to, way, row_to=row_to: to_core(level_to, row_to).wait_send())
    in_order(lambda level_to, way: to_row(level_to).wait_send())

    def sent(level_to, way):
        if way == 1:
            to_up(level_to).wait_send()
        if way == -1:
            to_down(level_to).wait_send()

    in_order(sent)


def sum_rows(parts, mixed, count):
    row_count, width = mixed.shape
    levels = count // 4
    inside = pl.BlockSpec(memory_space=pltpu.VMEM)

    def blocks(number):
        return pltpu.VMEM((number, row_count, width), jnp.bfloat16)

    return pl.pallas_call(
        functools.partial(sum_kernel, count),
        out_shape=jax.ShapeDtypeStruct(mixed.shape, jnp.float32),
        in_specs=[inside, inside],
        out_specs=inside,
        scratch_shapes=[
            blocks(count // 2),
            blocks(levels),
            blocks(levels),
            blocks(levels),
            blocks(levels),
            pltpu.SemaphoreType.DMA((2, count // 2)),
            pltpu.SemaphoreType.DMA((2, levels)),
            pltpu.SemaphoreType.DMA((2, levels)),
            pltpu.SemaphoreType.DMA((2, levels)),
        ],
        compiler_params=pltpu.CompilerParams(
            collective_id=1, has_side_effects=True, vmem_limit_bytes=56 * 2**20
        ),
    )(parts, mixed)


def expert_kernel(
    capacity, slots, top_count, aux, rows, gate, up, down, out, picks, scale, stacked, results
):
    step = pl.program_id(0)
    experts_local = stacked.shape[0]
    groups = stacked.shape[1]
    row_count = aux.shape[2]
    block_rows = row_count // 2
    width = 2 * row_count

    @pl.when(step == 0)
    def _():
        first = (lax.axis_index("tok") * experts_local).astype(jnp.float32)
        before = lax.broadcasted_iota(jnp.int32, (width, width), 0)
        after = lax.broadcasted_iota(jnp.int32, (width, width), 1)
        earlier = ((before < after) & (before // block_rows == after // block_rows)).astype(
            jnp.bfloat16
        )
        block = (lax.broadcasted_iota(jnp.int32, (1, width), 1) // block_rows) * capacity
        slot = lax.broadcasted_iota(jnp.int32, (slots, width), 0).astype(jnp.float32)

        @pl.loop(0, groups)
        def _(group):
            both = jnp.concatenate([aux[group * 2], aux[group * 2 + 1]], axis=1)
            ids, routes = both[:top_count], both[top_count:]
            for expert in range(experts_local):
                hit = (ids == first + expert).astype(jnp.float32)
                chosen = jnp.sum(hit, axis=0, keepdims=True)
                weight = jnp.sum(hit * routes, axis=0, keepdims=True)
                rank = jnp.dot(
                    jnp.broadcast_to(chosen, (16, width)).astype(jnp.bfloat16),
                    earlier,
                    preferred_element_type=jnp.float32,
                )[:1]
                target = jnp.where(chosen > 0.5, rank + block.astype(jnp.float32), -1.0)
                pick = (slot == target).astype(jnp.float32)
                picks[group, expert * slots : (expert + 1) * slots, :] = pick.astype(jnp.bfloat16)
                scale[expert, group] = jnp.sum(pick * weight, axis=1, keepdims=True)
            source = rows[pl.ds(pl.multiple_of(group * width, width), width), :]
            taken = jnp.dot(picks[group], source, preferred_element_type=jnp.float32)
            taken = taken.astype(jnp.bfloat16)
            for expert in range(experts_local):
                stacked[expert, group] = taken[expert * slots : (expert + 1) * slots]

    depth = stacked.shape[-1]
    inputs = stacked[step].reshape(groups * slots, depth)
    gate_part = jnp.dot(inputs, gate[0], preferred_element_type=jnp.float32)
    up_part = jnp.dot(inputs, up[0], preferred_element_type=jnp.float32)
    hidden = (gate_part / (1.0 + jnp.exp(-gate_part)) * up_part).astype(jnp.bfloat16)
    result = jnp.dot(hidden, down[0], preferred_element_type=jnp.float32)
    result = result * scale[step].reshape(groups * slots, 1)
    results[step] = result.astype(jnp.bfloat16).reshape(groups, slots, depth)

    @pl.when(step == experts_local - 1)
    def _():
        @pl.loop(0, groups)
        def _(group):
            value = jnp.concatenate([results[e, group] for e in range(experts_local)], axis=0)
            summed = lax.dot_general(
                picks[group], value, (((0,), (0,)), ((), ())), preferred_element_type=jnp.float32
            )
            out[pl.ds(pl.multiple_of(group * width, width), width), :] = summed.astype(
                jnp.bfloat16
            )


def run_experts(aux, rows, gate_weight, up_weight, down_weight, capacity):
    count, doubled, row_count = aux.shape
    experts_local, depth, hidden = gate_weight.shape
    groups = count // 2
    slots = -(-4 * capacity // 16) * 16
    whole = dict(pipeline_mode=pl.Buffered(1))
    return pl.pallas_call(
        functools.partial(expert_kernel, capacity, slots, doubled // 2),
        grid=(experts_local,),
        out_shape=jax.ShapeDtypeStruct(rows.shape, jnp.bfloat16),
        in_specs=[
            pl.BlockSpec(aux.shape, lambda e: (0, 0, 0), **whole),
            pl.BlockSpec(rows.shape, lambda e: (0, 0), **whole),
            pl.BlockSpec((1, depth, hidden), lambda e: (e, 0, 0)),
            pl.BlockSpec((1, depth, hidden), lambda e: (e, 0, 0)),
            pl.BlockSpec((1, hidden, depth), lambda e: (e, 0, 0)),
        ],
        out_specs=pl.BlockSpec(rows.shape, lambda e: (0, 0), **whole),
        scratch_shapes=[
            pltpu.VMEM((groups, experts_local * slots, 2 * row_count), jnp.bfloat16),
            pltpu.VMEM((experts_local, groups, slots, 1), jnp.float32),
            pltpu.VMEM((experts_local, groups, slots, depth), jnp.bfloat16),
            pltpu.VMEM((experts_local, groups, slots, depth), jnp.bfloat16),
        ],
        compiler_params=pltpu.CompilerParams(
            dimension_semantics=("arbitrary",), vmem_limit_bytes=62 * 2**20
        ),
    )(aux, rows, gate_weight, up_weight, down_weight)


def body(
    queries,
    new_keys,
    new_values,
    cache_keys,
    cache_values,
    cache_lens,
    residual,
    out_weight,
    norm_gain,
    expert_ids,
    route_weights,
    gate_weight,
    up_weight,
    down_weight,
):
    devices = lax.axis_size("tok")
    group = HEADS // KVH
    row_count = residual.shape[0]
    block_rows = row_count // 2
    top_count = expert_ids.shape[1]
    experts_local = gate_weight.shape[0]
    experts_all = experts_local * devices
    capacity = max(2, block_rows * top_count * 3 // (2 * experts_all))
    cache_rows = cache_keys.shape[0]
    length = cache_lens[0]
    key_all = jnp.concatenate([cache_keys, new_keys], 0).reshape(-1, KVH, HD).transpose(1, 0, 2)
    value_all = (
        jnp.concatenate([cache_values, new_values], 0).reshape(-1, KVH, HD).transpose(1, 0, 2)
    )
    place = lax.axis_index("tok")
    core = place % 2
    same_core = [list(range(parity, devices, 2)) for parity in range(2)]
    swap = [(i, i ^ 1) for i in range(devices)]
    groups = lax.axis_size("groups")
    part = lax.axis_index("groups")
    piece_rows = out_weight.shape[0] // groups
    piece = lax.dynamic_slice_in_dim(out_weight, part * piece_rows, piece_rows, 0)
    core_weight = lax.all_gather(
        piece, "tok", axis=0, tiled=True, axis_index_groups=same_core
    )
    positions = jnp.arange(row_count)
    cache_ok = jnp.broadcast_to(jnp.arange(cache_rows)[None, :] < length, (row_count, cache_rows))
    new_ok = jnp.arange(new_keys.shape[0])[None, :] <= positions[:, None]
    allowed = jnp.concatenate([cache_ok, new_ok], 1)
    shaped = queries.reshape(row_count, KVH, group, HD).transpose(1, 0, 2, 3)
    output = head_attention(shaped, key_all, value_all, allowed)
    attended = output.transpose(1, 0, 2, 3).reshape(
        row_count, devices // 2, 2, groups, piece_rows
    )
    own_columns = lax.dynamic_index_in_dim(attended, core, 2, keepdims=False)
    other_columns = lax.dynamic_index_in_dim(attended, 1 - core, 2, keepdims=False)
    sibling_columns = lax.ppermute(other_columns, "tok", swap)
    both = jnp.concatenate([own_columns, sibling_columns], 0)
    projected = []
    for step in range(groups):
        rows = lax.dynamic_index_in_dim(both, (part + step) % groups, 2, keepdims=False)
        rows = rows.reshape(2 * row_count, -1)
        if step:
            ahead = [(i, (i + step) % groups) for i in range(groups)]
            rows = lax.ppermute(rows, "groups", ahead)
        projected.append(jnp.dot(rows, core_weight, preferred_element_type=jnp.float32))
    mixed = residual.astype(jnp.float32)
    for step in reversed(range(groups)):
        from_sibling = lax.ppermute(
            projected[step][row_count:].astype(jnp.bfloat16), "tok", swap
        )
        summed_rows = projected[step][:row_count] + from_sibling.astype(jnp.float32)
        if step:
            back = [(i, (i - step) % groups) for i in range(groups)]
            summed_rows = lax.ppermute(summed_rows.astype(jnp.bfloat16), "groups", back)
        mixed = mixed + summed_rows.astype(jnp.float32)
    factor = lax.rsqrt(jnp.mean(mixed * mixed, axis=-1, keepdims=True) + 1e-06)
    normed = (mixed * factor * norm_gain).astype(jnp.bfloat16)
    aux = jnp.concatenate([expert_ids.astype(jnp.float32).T, route_weights.T], axis=0)
    all_rows, all_aux = gather_rows(normed, aux, devices)
    summed = run_experts(
        all_aux,
        all_rows.reshape(devices * row_count, -1),
        gate_weight,
        up_weight,
        down_weight,
        capacity,
    )
    final = sum_rows(summed.reshape(devices, row_count, -1), mixed, devices)
    return final.astype(jnp.bfloat16)


def solution(mesh):
    placed = (
        P(("groups", "tok"), None),
        P(("groups", "tok"), None),
        P(("groups", "tok"), None),
        P(("groups", "tok"), None),
        P(("groups", "tok"), None),
        P(("groups", "tok")),
        P(("groups", "tok"), None),
        P("tok", None),
        P(),
        P(("groups", "tok"), None),
        P(("groups", "tok"), None),
        P("tok", None, None),
        P("tok", None, None),
        P("tok", None, None),
    )
    return jax.shard_map(
        body, mesh=mesh, in_specs=placed, out_specs=P(("groups", "tok"), None), check_vma=False
    )
```

```python
import jax
import jax.numpy as jnp
import functools

from jax import lax
from jax.experimental import pallas as pl
from jax.experimental.pallas import tpu as pltpu
from jax.sharding import PartitionSpec as P

MESH = pl.DeviceIdType.MESH

HEADS = 32
KVH = 4
HD = 128


def head_attention(query_rows, key_rows, value_rows, allowed):

    def one_head(operands):
        query_head, key_head, value_head = operands
        scores = jnp.einsum("rgd,kd->rgk", query_head, key_head, preferred_element_type=jnp.float32)
        scores = scores * query_head.shape[-1] ** (-0.5)
        scores = jnp.where(allowed[:, None, :], scores, -1e30)
        highest = jnp.max(scores, axis=-1, keepdims=True)
        weights = jnp.exp(scores - highest)
        weights = (weights / jnp.sum(weights, axis=-1, keepdims=True)).astype(jnp.bfloat16)
        return jnp.einsum(
            "rgk,kd->rgd", weights, value_head, preferred_element_type=jnp.float32
        ).astype(jnp.bfloat16)

    return lax.map(one_head, (query_rows, key_rows, value_rows))


def place_of(count):
    place = lax.axis_index("tok")
    return place // 4, (place // 2) % 2, place % 2, count // 4


def greet(level, row, core, levels):
    barrier = pltpu.get_barrier_semaphore()

    def tell(level_to, row_to, core_to):
        pl.semaphore_signal(
            barrier,
            inc=1,
            device_id={"tok": (level_to * 2 + row_to) * 2 + core_to},
            device_id_type=MESH,
        )

    tell(level, 1 - row, core)
    tell(level, row, 1 - core)

    @pl.when(level > 0)
    def _():
        tell(level - 1, row, core)

    @pl.when(level < levels - 1)
    def _():
        tell(level + 1, row, core)

    ends = (level > 0).astype(jnp.int32) + (level < levels - 1).astype(jnp.int32)
    pl.semaphore_wait(barrier, 2 + ends)


def gather_kernel(count, rows_ref, aux_ref, all_rows, all_aux, own_sem, send_sem, recv_sem):
    level, row, core, levels = place_of(count)
    greet(level, row, core, levels)
    me = lax.axis_index("tok")

    def sends(block, way, target, first):
        out = []
        pairs = ((rows_ref, all_rows), (aux_ref, all_aux))
        for which, (own, everyone) in enumerate(pairs):
            out.append(
                pltpu.make_async_remote_copy(
                    src_ref=own if first else everyone.at[block],
                    dst_ref=everyone.at[block],
                    send_sem=send_sem.at[which, way, block],
                    recv_sem=recv_sem.at[which, block],
                    device_id={"tok": target},
                    device_id_type=MESH,
                )
            )
        return out

    def each(block, act, first=False, up=None, down=None, across=True):
        if up is not None:
            @pl.when(up)
            def _():
                for copy in sends(block, 0, me + 4, first):
                    act(copy)
        if down is not None:
            @pl.when(down)
            def _():
                for copy in sends(block, 1, me - 4, first):
                    act(copy)
        if across:
            for copy in sends(block, 2, (level * 2 + 1 - row) * 2 + core, first):
                act(copy)
        for copy in sends(block, 3, (level * 2 + row) * 2 + 1 - core, first):
            act(copy)

    def arrived(block):
        for copy in sends(block, 3, (level * 2 + row) * 2 + 1 - core, False):
            copy.wait_recv()

    start = lambda copy: copy.start()
    done = lambda copy: copy.wait_send()
    can_up, can_down = level < levels - 1, level > 0

    def line_step(distance, act, receive):
        @pl.when(level >= distance)
        def _():
            block = me - 4 * distance
            if receive:
                arrived(block)
            each(block, act, up=can_up)

        @pl.when(level + distance < levels)
        def _():
            block = me + 4 * distance
            if receive:
                arrived(block)
            each(block, act, down=can_down)

    def row_step(distance, act, receive):
        def one(level_from):
            block = (level_from * 2 + 1 - row) * 2 + core
            if receive:
                arrived(block)
            each(block, act, across=False)

        if distance == 0:
            one(level)
        else:
            @pl.when(level >= distance)
            def _():
                one(level - distance)

            @pl.when(level + distance < levels)
            def _():
                one(level + distance)

    each(me, start, first=True, up=can_up, down=can_down)
    own_rows = pltpu.make_async_copy(rows_ref, all_rows.at[me], own_sem.at[0])
    own_aux = pltpu.make_async_copy(aux_ref, all_aux.at[me], own_sem.at[1])
    own_rows.start()
    own_aux.start()
    for step in range(1, levels + 1):
        if step < levels:
            line_step(step, start, True)
        row_step(step - 1, start, True)
    for index in range(count // 2):
        arrived(index * 2 + 1 - core)
    each(me, done, first=True, up=can_up, down=can_down)
    for step in range(1, levels):
        line_step(step, done, False)
    for step in range(levels):
        row_step(step, done, False)
    own_rows.wait()
    own_aux.wait()


def gather_rows(rows, aux, count):
    anywhere = pl.BlockSpec(memory_space=pl.ANY)
    return pl.pallas_call(
        functools.partial(gather_kernel, count),
        out_shape=(
            jax.ShapeDtypeStruct((count,) + rows.shape, rows.dtype),
            jax.ShapeDtypeStruct((count,) + aux.shape, aux.dtype),
        ),
        in_specs=[anywhere, anywhere],
        out_specs=(anywhere, anywhere),
        scratch_shapes=[
            pltpu.SemaphoreType.DMA((2,)),
            pltpu.SemaphoreType.DMA((2, 4, count)),
            pltpu.SemaphoreType.DMA((2, count)),
        ],
        compiler_params=pltpu.CompilerParams(collective_id=0, has_side_effects=True),
    )(rows, aux)


def sum_kernel(
    count, parts, mixed, out, held, from_core, from_row, total, from_below, from_above,
    core_sem, row_sem, up_sem, down_sem,
):
    level, row, core, levels = place_of(count)
    greet(level, row, core, levels)
    me = lax.axis_index("tok")
    row_count = mixed.shape[0]
    tile = 16

    def tiles(act):
        @pl.loop(0, row_count // tile)
        def _(index):
            act(pl.ds(pl.multiple_of(index * tile, tile), tile))

    def remote(src, dst, sems, index, target):
        return pltpu.make_async_remote_copy(
            src_ref=src,
            dst_ref=dst,
            send_sem=sems.at[0, index],
            recv_sem=sems.at[1, index],
            device_id={"tok": target},
            device_id_type=MESH,
        )

    def to_core(level_to, row_to):
        slot = level_to * 2 + row_to
        target = (level * 2 + row) * 2 + 1 - core
        return remote(parts.at[slot * 2 + 1 - core], from_core.at[slot], core_sem, slot, target)

    def to_row(level_to):
        target = (level * 2 + 1 - row) * 2 + core
        slot = level_to * 2 + 1 - row
        return remote(from_core.at[slot], from_row.at[level_to], row_sem, level_to, target)

    def to_up(level_to):
        return remote(total.at[level_to], from_below.at[level_to], up_sem, level_to, me + 4)

    def to_down(level_to):
        return remote(total.at[level_to], from_above.at[level_to], down_sem, level_to, me - 4)

    def in_order(act):
        for step in range(levels - 1):
            high, low = levels - 1 - step, step

            @pl.when(high > level)
            def _():
                act(high, 1)

            @pl.when(low < level)
            def _():
                act(low, -1)

        act(level, 0)

    for row_to in (1 - row, row):
        in_order(lambda level_to, way, row_to=row_to: to_core(level_to, row_to).start())

    def pass_row(level_to, way):
        slot = level_to * 2 + 1 - row
        to_core(level_to, 1 - row).wait_recv()

        def add(where):
            both = parts[slot * 2 + core, where, :].astype(jnp.float32) + from_core[
                slot, where, :
            ].astype(jnp.float32)
            from_core[slot, where, :] = both.astype(jnp.bfloat16)

        tiles(add)
        to_row(level_to).start()

    in_order(pass_row)

    def base(slot, level_to, where):
        return (
            parts[slot * 2 + core, where, :].astype(jnp.float32)
            + from_core[slot, where, :].astype(jnp.float32)
            + from_row[level_to, where, :].astype(jnp.float32)
        )

    def pass_line(level_to, way):
        slot = level_to * 2 + row
        to_core(level_to, row).wait_recv()
        to_row(level_to).wait_recv()
        if way == 0:
            def keep(where):
                total[level_to, where, :] = base(slot, level_to, where).astype(jnp.bfloat16)

            def finish(where):
                held[where, :] = mixed[where, :] + base(slot, level_to, where)

            tiles(finish)
            for neighbour, incoming, copy in (
                (level > 0, from_below, to_up),
                (level < levels - 1, from_above, to_down),
            ):
                @pl.when(neighbour)
                def _(incoming=incoming, copy=copy):
                    copy(level_to).wait_recv()

                    def more(where):
                        held[where, :] += incoming[level_to, where, :].astype(jnp.float32)

                    tiles(more)

            def rounded(where):
                out[where, :] = held[where, :].astype(out.dtype)

            tiles(rounded)
            return
        behind = level > 0 if way == 1 else level < levels - 1
        incoming, copy = (from_below, to_up) if way == 1 else (from_above, to_down)

        @pl.when(behind)
        def _():
            copy(level_to).wait_recv()

            def add(where):
                value = base(slot, level_to, where) + incoming[level_to, where, :].astype(
                    jnp.float32
                )
                total[level_to, where, :] = value.astype(jnp.bfloat16)

            tiles(add)

        @pl.when(jnp.logical_not(behind))
        def _():
            def add(where):
                total[level_to, where, :] = base(slot, level_to, where).astype(jnp.bfloat16)

            tiles(add)

        copy(level_to).start()

    in_order(pass_line)
    for row_to in (1 - row, row):
        in_order(lambda level_to, way, row_to=row_to: to_core(level_to, row_to).wait_send())
    in_order(lambda level_to, way: to_row(level_to).wait_send())

    def sent(level_to, way):
        if way == 1:
            to_up(level_to).wait_send()
        if way == -1:
            to_down(level_to).wait_send()

    in_order(sent)


def sum_rows(parts, mixed, count):
    row_count, width = mixed.shape
    levels = count // 4
    inside = pl.BlockSpec(memory_space=pltpu.VMEM)

    def blocks(number):
        return pltpu.VMEM((number, row_count, width), jnp.bfloat16)

    return pl.pallas_call(
        functools.partial(sum_kernel, count),
        out_shape=jax.ShapeDtypeStruct(mixed.shape, jnp.bfloat16),
        in_specs=[inside, inside],
        out_specs=inside,
        scratch_shapes=[
            pltpu.VMEM(mixed.shape, jnp.float32),
            blocks(count // 2),
            blocks(levels),
            blocks(levels),
            blocks(levels),
            blocks(levels),
            pltpu.SemaphoreType.DMA((2, count // 2)),
            pltpu.SemaphoreType.DMA((2, levels)),
            pltpu.SemaphoreType.DMA((2, levels)),
            pltpu.SemaphoreType.DMA((2, levels)),
        ],
        compiler_params=pltpu.CompilerParams(
            collective_id=1, has_side_effects=True, vmem_limit_bytes=56 * 2**20
        ),
    )(parts, mixed)


def expert_kernel(
    capacity, slots, top_count, aux, rows, gate, up, down, out, picks, scale, stacked, results
):
    step = pl.program_id(0)
    experts_local = stacked.shape[0]
    groups = stacked.shape[1]
    row_count = aux.shape[2]
    block_rows = row_count // 2
    width = 2 * row_count

    @pl.when(step == 0)
    def _():
        first = (lax.axis_index("tok") * experts_local).astype(jnp.float32)
        before = lax.broadcasted_iota(jnp.int32, (width, width), 0)
        after = lax.broadcasted_iota(jnp.int32, (width, width), 1)
        earlier = ((before < after) & (before // block_rows == after // block_rows)).astype(
            jnp.bfloat16
        )
        block = (lax.broadcasted_iota(jnp.int32, (1, width), 1) // block_rows) * capacity
        slot = lax.broadcasted_iota(jnp.int32, (slots, width), 0).astype(jnp.float32)

        @pl.loop(0, groups)
        def _(group):
            both = jnp.concatenate([aux[group * 2], aux[group * 2 + 1]], axis=1)
            ids, routes = both[:top_count], both[top_count:]
            for expert in range(experts_local):
                hit = (ids == first + expert).astype(jnp.float32)
                chosen = jnp.sum(hit, axis=0, keepdims=True)
                weight = jnp.sum(hit * routes, axis=0, keepdims=True)
                rank = jnp.dot(
                    jnp.broadcast_to(chosen, (16, width)).astype(jnp.bfloat16),
                    earlier,
                    preferred_element_type=jnp.float32,
                )[:1]
                target = jnp.where(chosen > 0.5, rank + block.astype(jnp.float32), -1.0)
                pick = (slot == target).astype(jnp.float32)
                picks[group, expert * slots : (expert + 1) * slots, :] = pick.astype(jnp.bfloat16)
                scale[expert, group] = jnp.sum(pick * weight, axis=1, keepdims=True)
            source = rows[pl.ds(pl.multiple_of(group * width, width), width), :]
            taken = jnp.dot(picks[group], source, preferred_element_type=jnp.float32)
            taken = taken.astype(jnp.bfloat16)
            for expert in range(experts_local):
                stacked[expert, group] = taken[expert * slots : (expert + 1) * slots]

    depth = stacked.shape[-1]
    inputs = stacked[step].reshape(groups * slots, depth)
    gate_part = jnp.dot(inputs, gate[0], preferred_element_type=jnp.float32)
    up_part = jnp.dot(inputs, up[0], preferred_element_type=jnp.float32)
    hidden = (gate_part / (1.0 + jnp.exp(-gate_part)) * up_part).astype(jnp.bfloat16)
    result = jnp.dot(hidden, down[0], preferred_element_type=jnp.float32)
    result = result * scale[step].reshape(groups * slots, 1)
    results[step] = result.astype(jnp.bfloat16).reshape(groups, slots, depth)

    @pl.when(step == experts_local - 1)
    def _():
        @pl.loop(0, groups)
        def _(group):
            value = jnp.concatenate([results[e, group] for e in range(experts_local)], axis=0)
            summed = lax.dot_general(
                picks[group], value, (((0,), (0,)), ((), ())), preferred_element_type=jnp.float32
            )
            out[pl.ds(pl.multiple_of(group * width, width), width), :] = summed.astype(
                jnp.bfloat16
            )


def run_experts(aux, rows, gate_weight, up_weight, down_weight, capacity):
    count, doubled, row_count = aux.shape
    experts_local, depth, hidden = gate_weight.shape
    groups = count // 2
    slots = -(-4 * capacity // 16) * 16
    whole = dict(pipeline_mode=pl.Buffered(1))
    return pl.pallas_call(
        functools.partial(expert_kernel, capacity, slots, doubled // 2),
        grid=(experts_local,),
        out_shape=jax.ShapeDtypeStruct(rows.shape, jnp.bfloat16),
        in_specs=[
            pl.BlockSpec(aux.shape, lambda e: (0, 0, 0), **whole),
            pl.BlockSpec(rows.shape, lambda e: (0, 0), **whole),
            pl.BlockSpec((1, depth, hidden), lambda e: (e, 0, 0)),
            pl.BlockSpec((1, depth, hidden), lambda e: (e, 0, 0)),
            pl.BlockSpec((1, hidden, depth), lambda e: (e, 0, 0)),
        ],
        out_specs=pl.BlockSpec(rows.shape, lambda e: (0, 0), **whole),
        scratch_shapes=[
            pltpu.VMEM((groups, experts_local * slots, 2 * row_count), jnp.bfloat16),
            pltpu.VMEM((experts_local, groups, slots, 1), jnp.float32),
            pltpu.VMEM((experts_local, groups, slots, depth), jnp.bfloat16),
            pltpu.VMEM((experts_local, groups, slots, depth), jnp.bfloat16),
        ],
        compiler_params=pltpu.CompilerParams(
            dimension_semantics=("arbitrary",), vmem_limit_bytes=62 * 2**20
        ),
    )(aux, rows, gate_weight, up_weight, down_weight)


def body(
    queries,
    new_keys,
    new_values,
    cache_keys,
    cache_values,
    cache_lens,
    residual,
    out_weight,
    norm_gain,
    expert_ids,
    route_weights,
    gate_weight,
    up_weight,
    down_weight,
):
    devices = lax.axis_size("tok")
    group = HEADS // KVH
    row_count = residual.shape[0]
    block_rows = row_count // 2
    top_count = expert_ids.shape[1]
    experts_local = gate_weight.shape[0]
    experts_all = experts_local * devices
    capacity = max(2, block_rows * top_count * 3 // (2 * experts_all))
    cache_rows = cache_keys.shape[0]
    length = cache_lens[0]
    key_all = jnp.concatenate([cache_keys, new_keys], 0).reshape(-1, KVH, HD).transpose(1, 0, 2)
    value_all = (
        jnp.concatenate([cache_values, new_values], 0).reshape(-1, KVH, HD).transpose(1, 0, 2)
    )
    place = lax.axis_index("tok")
    core = place % 2
    same_core = [list(range(parity, devices, 2)) for parity in range(2)]
    swap = [(i, i ^ 1) for i in range(devices)]
    groups = lax.axis_size("groups")
    part = lax.axis_index("groups")
    piece_rows = out_weight.shape[0] // groups
    piece = lax.dynamic_slice_in_dim(out_weight, part * piece_rows, piece_rows, 0)
    core_weight = lax.all_gather(
        piece, "tok", axis=0, tiled=True, axis_index_groups=same_core
    )
    positions = jnp.arange(row_count)
    cache_ok = jnp.broadcast_to(jnp.arange(cache_rows)[None, :] < length, (row_count, cache_rows))
    new_ok = jnp.arange(new_keys.shape[0])[None, :] <= positions[:, None]
    allowed = jnp.concatenate([cache_ok, new_ok], 1)
    shaped = queries.reshape(row_count, KVH, group, HD).transpose(1, 0, 2, 3)
    output = head_attention(shaped, key_all, value_all, allowed)
    attended = output.transpose(1, 0, 2, 3).reshape(
        row_count, devices // 2, 2, groups, piece_rows
    )
    own_columns = lax.dynamic_index_in_dim(attended, core, 2, keepdims=False)
    other_columns = lax.dynamic_index_in_dim(attended, 1 - core, 2, keepdims=False)
    sibling_columns = lax.ppermute(other_columns, "tok", swap)
    both = jnp.concatenate([own_columns, sibling_columns], 0)
    projected = []
    for step in range(groups):
        rows = lax.dynamic_index_in_dim(both, (part + step) % groups, 2, keepdims=False)
        rows = rows.reshape(2 * row_count, -1)
        if step:
            ahead = [(i, (i + step) % groups) for i in range(groups)]
            rows = lax.ppermute(rows, "groups", ahead)
        projected.append(jnp.dot(rows, core_weight, preferred_element_type=jnp.float32))
    mixed = residual.astype(jnp.float32)
    for step in reversed(range(groups)):
        from_sibling = lax.ppermute(
            projected[step][row_count:].astype(jnp.bfloat16), "tok", swap
        )
        summed_rows = projected[step][:row_count] + from_sibling.astype(jnp.float32)
        if step:
            back = [(i, (i - step) % groups) for i in range(groups)]
            summed_rows = lax.ppermute(summed_rows.astype(jnp.bfloat16), "groups", back)
        mixed = mixed + summed_rows.astype(jnp.float32)
    factor = lax.rsqrt(jnp.mean(mixed * mixed, axis=-1, keepdims=True) + 1e-06)
    normed = (mixed * factor * norm_gain).astype(jnp.bfloat16)
    aux = jnp.concatenate([expert_ids.astype(jnp.float32).T, route_weights.T], axis=0)
    all_rows, all_aux = gather_rows(normed, aux, devices)
    summed = run_experts(
        all_aux,
        all_rows.reshape(devices * row_count, -1),
        gate_weight,
        up_weight,
        down_weight,
        capacity,
    )
    return sum_rows(summed.reshape(devices, row_count, -1), mixed, devices)


def solution(mesh):
    placed = (
        P(("groups", "tok"), None),
        P(("groups", "tok"), None),
        P(("groups", "tok"), None),
        P(("groups", "tok"), None),
        P(("groups", "tok"), None),
        P(("groups", "tok")),
        P(("groups", "tok"), None),
        P("tok", None),
        P(),
        P(("groups", "tok"), None),
        P(("groups", "tok"), None),
        P("tok", None, None),
        P("tok", None, None),
        P("tok", None, None),
    )
    return jax.shard_map(
        body, mesh=mesh, in_specs=placed, out_specs=P(("groups", "tok"), None), check_vma=False
    )
```

```python
import jax
import jax.numpy as jnp
import functools

from jax import lax
from jax.experimental import pallas as pl
from jax.experimental.pallas import tpu as pltpu
from jax.sharding import PartitionSpec as P

MESH = pl.DeviceIdType.MESH

HEADS = 32
KVH = 4
HD = 128


def head_attention(query_rows, key_rows, value_rows, allowed):

    def one_head(operands):
        query_head, key_head, value_head = operands
        scores = jnp.einsum("rgd,kd->rgk", query_head, key_head, preferred_element_type=jnp.float32)
        scores = scores * query_head.shape[-1] ** (-0.5)
        scores = jnp.where(allowed[:, None, :], scores, -1e30)
        highest = jnp.max(scores, axis=-1, keepdims=True)
        weights = jnp.exp(scores - highest)
        weights = (weights / jnp.sum(weights, axis=-1, keepdims=True)).astype(jnp.bfloat16)
        return jnp.einsum(
            "rgk,kd->rgd", weights, value_head, preferred_element_type=jnp.float32
        ).astype(jnp.bfloat16)

    return lax.map(one_head, (query_rows, key_rows, value_rows))


def place_of(count):
    place = lax.axis_index("tok")
    return place // 4, (place // 2) % 2, place % 2, count // 4


def greet(level, row, core, levels):
    barrier = pltpu.get_barrier_semaphore()

    def tell(level_to, row_to, core_to):
        pl.semaphore_signal(
            barrier,
            inc=1,
            device_id={"tok": (level_to * 2 + row_to) * 2 + core_to},
            device_id_type=MESH,
        )

    tell(level, 1 - row, core)
    tell(level, row, 1 - core)

    @pl.when(level > 0)
    def _():
        tell(level - 1, row, core)

    @pl.when(level < levels - 1)
    def _():
        tell(level + 1, row, core)

    ends = (level > 0).astype(jnp.int32) + (level < levels - 1).astype(jnp.int32)
    pl.semaphore_wait(barrier, 2 + ends)


def gather_kernel(count, rows_ref, aux_ref, all_rows, all_aux, own_sem, send_sem, recv_sem):
    level, row, core, levels = place_of(count)
    greet(level, row, core, levels)
    me = lax.axis_index("tok")

    def sends(block, way, target, first):
        out = []
        pairs = ((rows_ref, all_rows), (aux_ref, all_aux))
        for which, (own, everyone) in enumerate(pairs):
            out.append(
                pltpu.make_async_remote_copy(
                    src_ref=own if first else everyone.at[block],
                    dst_ref=everyone.at[block],
                    send_sem=send_sem.at[which, way, block],
                    recv_sem=recv_sem.at[which, block],
                    device_id={"tok": target},
                    device_id_type=MESH,
                )
            )
        return out

    def each(block, act, first=False, up=None, down=None, across=True):
        if up is not None:
            @pl.when(up)
            def _():
                for copy in sends(block, 0, me + 4, first):
                    act(copy)
        if down is not None:
            @pl.when(down)
            def _():
                for copy in sends(block, 1, me - 4, first):
                    act(copy)
        if across:
            for copy in sends(block, 2, (level * 2 + 1 - row) * 2 + core, first):
                act(copy)
        for copy in sends(block, 3, (level * 2 + row) * 2 + 1 - core, first):
            act(copy)

    def arrived(block):
        for copy in sends(block, 3, (level * 2 + row) * 2 + 1 - core, False):
            copy.wait_recv()

    start = lambda copy: copy.start()
    done = lambda copy: copy.wait_send()
    can_up, can_down = level < levels - 1, level > 0

    def line_step(distance, act, receive):
        @pl.when(level >= distance)
        def _():
            block = me - 4 * distance
            if receive:
                arrived(block)
            each(block, act, up=can_up)

        @pl.when(level + distance < levels)
        def _():
            block = me + 4 * distance
            if receive:
                arrived(block)
            each(block, act, down=can_down)

    def row_step(distance, act, receive):
        def one(level_from):
            block = (level_from * 2 + 1 - row) * 2 + core
            if receive:
                arrived(block)
            each(block, act, across=False)

        if distance == 0:
            one(level)
        else:
            @pl.when(level >= distance)
            def _():
                one(level - distance)

            @pl.when(level + distance < levels)
            def _():
                one(level + distance)

    each(me, start, first=True, up=can_up, down=can_down)
    own_rows = pltpu.make_async_copy(rows_ref, all_rows.at[me], own_sem.at[0])
    own_aux = pltpu.make_async_copy(aux_ref, all_aux.at[me], own_sem.at[1])
    own_rows.start()
    own_aux.start()
    for step in range(1, levels + 1):
        if step < levels:
            line_step(step, start, True)
        row_step(step - 1, start, True)
    for index in range(count // 2):
        arrived(index * 2 + 1 - core)
    each(me, done, first=True, up=can_up, down=can_down)
    for step in range(1, levels):
        line_step(step, done, False)
    for step in range(levels):
        row_step(step, done, False)
    own_rows.wait()
    own_aux.wait()


def gather_rows(rows, aux, count):
    anywhere = pl.BlockSpec(memory_space=pl.ANY)
    return pl.pallas_call(
        functools.partial(gather_kernel, count),
        out_shape=(
            jax.ShapeDtypeStruct((count,) + rows.shape, rows.dtype),
            jax.ShapeDtypeStruct((count,) + aux.shape, aux.dtype),
        ),
        in_specs=[anywhere, anywhere],
        out_specs=(anywhere, anywhere),
        scratch_shapes=[
            pltpu.SemaphoreType.DMA((2,)),
            pltpu.SemaphoreType.DMA((2, 4, count)),
            pltpu.SemaphoreType.DMA((2, count)),
        ],
        compiler_params=pltpu.CompilerParams(collective_id=0, has_side_effects=True),
    )(rows, aux)


def sum_kernel(
    count, parts, mixed, out, held, from_core, from_row, total, from_below, from_above,
    core_sem, row_sem, up_sem, down_sem,
):
    level, row, core, levels = place_of(count)
    greet(level, row, core, levels)
    me = lax.axis_index("tok")
    row_count = mixed.shape[0]
    tile = 16

    def tiles(act):
        @pl.loop(0, row_count // tile)
        def _(index):
            act(pl.ds(pl.multiple_of(index * tile, tile), tile))

    def remote(src, dst, sems, index, target):
        return pltpu.make_async_remote_copy(
            src_ref=src,
            dst_ref=dst,
            send_sem=sems.at[0, index],
            recv_sem=sems.at[1, index],
            device_id={"tok": target},
            device_id_type=MESH,
        )

    def to_core(level_to, row_to):
        slot = level_to * 2 + row_to
        target = (level * 2 + row) * 2 + 1 - core
        return remote(parts.at[slot * 2 + 1 - core], from_core.at[slot], core_sem, slot, target)

    def to_row(level_to):
        target = (level * 2 + 1 - row) * 2 + core
        slot = level_to * 2 + 1 - row
        return remote(from_core.at[slot], from_row.at[level_to], row_sem, level_to, target)

    def to_up(level_to):
        return remote(total.at[level_to], from_below.at[level_to], up_sem, level_to, me + 4)

    def to_down(level_to):
        return remote(total.at[level_to], from_above.at[level_to], down_sem, level_to, me - 4)

    def in_order(act):
        for step in range(levels - 1):
            high, low = levels - 1 - step, step

            @pl.when(high > level)
            def _():
                act(high, 1)

            @pl.when(low < level)
            def _():
                act(low, -1)

        act(level, 0)

    in_order(lambda level_to, way: to_core(level_to, 1 - row).start())

    def pass_row(level_to, way):
        slot = level_to * 2 + 1 - row
        to_core(level_to, 1 - row).wait_recv()

        def add(where):
            both = parts[slot * 2 + core, where, :].astype(jnp.float32) + from_core[
                slot, where, :
            ].astype(jnp.float32)
            from_core[slot, where, :] = both.astype(jnp.bfloat16)

        tiles(add)
        to_row(level_to).start()
        to_core(level_to, row).start()

    in_order(pass_row)

    def base(slot, level_to, where):
        return (
            parts[slot * 2 + core, where, :].astype(jnp.float32)
            + from_core[slot, where, :].astype(jnp.float32)
            + from_row[level_to, where, :].astype(jnp.float32)
        )

    def pass_line(level_to, way):
        slot = level_to * 2 + row
        to_core(level_to, row).wait_recv()
        to_row(level_to).wait_recv()
        if way == 0:
            def keep(where):
                total[level_to, where, :] = base(slot, level_to, where).astype(jnp.bfloat16)

            def finish(where):
                held[where, :] = mixed[where, :] + base(slot, level_to, where)

            tiles(finish)
            for neighbour, incoming, copy in (
                (level > 0, from_below, to_up),
                (level < levels - 1, from_above, to_down),
            ):
                @pl.when(neighbour)
                def _(incoming=incoming, copy=copy):
                    copy(level_to).wait_recv()

                    def more(where):
                        held[where, :] += incoming[level_to, where, :].astype(jnp.float32)

                    tiles(more)

            def rounded(where):
                out[where, :] = held[where, :].astype(out.dtype)

            tiles(rounded)
            return
        behind = level > 0 if way == 1 else level < levels - 1
        incoming, copy = (from_below, to_up) if way == 1 else (from_above, to_down)

        @pl.when(behind)
        def _():
            copy(level_to).wait_recv()

            def add(where):
                value = base(slot, level_to, where) + incoming[level_to, where, :].astype(
                    jnp.float32
                )
                total[level_to, where, :] = value.astype(jnp.bfloat16)

            tiles(add)

        @pl.when(jnp.logical_not(behind))
        def _():
            def add(where):
                total[level_to, where, :] = base(slot, level_to, where).astype(jnp.bfloat16)

            tiles(add)

        copy(level_to).start()

    in_order(pass_line)
    for row_to in (1 - row, row):
        in_order(lambda level_to, way, row_to=row_to: to_core(level_to, row_to).wait_send())
    in_order(lambda level_to, way: to_row(level_to).wait_send())

    def sent(level_to, way):
        if way == 1:
            to_up(level_to).wait_send()
        if way == -1:
            to_down(level_to).wait_send()

    in_order(sent)


def sum_rows(parts, mixed, count):
    row_count, width = mixed.shape
    levels = count // 4
    inside = pl.BlockSpec(memory_space=pltpu.VMEM)

    def blocks(number):
        return pltpu.VMEM((number, row_count, width), jnp.bfloat16)

    return pl.pallas_call(
        functools.partial(sum_kernel, count),
        out_shape=jax.ShapeDtypeStruct(mixed.shape, jnp.bfloat16),
        in_specs=[inside, inside],
        out_specs=inside,
        scratch_shapes=[
            pltpu.VMEM(mixed.shape, jnp.float32),
            blocks(count // 2),
            blocks(levels),
            blocks(levels),
            blocks(levels),
            blocks(levels),
            pltpu.SemaphoreType.DMA((2, count // 2)),
            pltpu.SemaphoreType.DMA((2, levels)),
            pltpu.SemaphoreType.DMA((2, levels)),
            pltpu.SemaphoreType.DMA((2, levels)),
        ],
        compiler_params=pltpu.CompilerParams(
            collective_id=1, has_side_effects=True, vmem_limit_bytes=56 * 2**20
        ),
    )(parts, mixed)


def expert_kernel(
    capacity, slots, top_count, aux, rows, gate, up, down, out, picks, scale, stacked, results
):
    step = pl.program_id(0)
    experts_local = stacked.shape[0]
    groups = stacked.shape[1]
    row_count = aux.shape[2]
    block_rows = row_count // 2
    width = 2 * row_count

    @pl.when(step == 0)
    def _():
        first = (lax.axis_index("tok") * experts_local).astype(jnp.float32)
        before = lax.broadcasted_iota(jnp.int32, (width, width), 0)
        after = lax.broadcasted_iota(jnp.int32, (width, width), 1)
        earlier = ((before < after) & (before // block_rows == after // block_rows)).astype(
            jnp.bfloat16
        )
        block = (lax.broadcasted_iota(jnp.int32, (1, width), 1) // block_rows) * capacity
        slot = lax.broadcasted_iota(jnp.int32, (slots, width), 0).astype(jnp.float32)

        @pl.loop(0, groups)
        def _(group):
            both = jnp.concatenate([aux[group * 2], aux[group * 2 + 1]], axis=1)
            ids, routes = both[:top_count], both[top_count:]
            for expert in range(experts_local):
                hit = (ids == first + expert).astype(jnp.float32)
                chosen = jnp.sum(hit, axis=0, keepdims=True)
                weight = jnp.sum(hit * routes, axis=0, keepdims=True)
                rank = jnp.dot(
                    jnp.broadcast_to(chosen, (16, width)).astype(jnp.bfloat16),
                    earlier,
                    preferred_element_type=jnp.float32,
                )[:1]
                target = jnp.where(chosen > 0.5, rank + block.astype(jnp.float32), -1.0)
                pick = (slot == target).astype(jnp.float32)
                picks[group, expert * slots : (expert + 1) * slots, :] = pick.astype(jnp.bfloat16)
                scale[expert, group] = jnp.sum(pick * weight, axis=1, keepdims=True)
            source = rows[pl.ds(pl.multiple_of(group * width, width), width), :]
            taken = jnp.dot(picks[group], source, preferred_element_type=jnp.float32)
            taken = taken.astype(jnp.bfloat16)
            for expert in range(experts_local):
                stacked[expert, group] = taken[expert * slots : (expert + 1) * slots]

    depth = stacked.shape[-1]
    inputs = stacked[step].reshape(groups * slots, depth)
    gate_part = jnp.dot(inputs, gate[0], preferred_element_type=jnp.float32)
    up_part = jnp.dot(inputs, up[0], preferred_element_type=jnp.float32)
    hidden = (gate_part / (1.0 + jnp.exp(-gate_part)) * up_part).astype(jnp.bfloat16)
    result = jnp.dot(hidden, down[0], preferred_element_type=jnp.float32)
    result = result * scale[step].reshape(groups * slots, 1)
    results[step] = result.astype(jnp.bfloat16).reshape(groups, slots, depth)

    @pl.when(step == experts_local - 1)
    def _():
        @pl.loop(0, groups)
        def _(group):
            value = jnp.concatenate([results[e, group] for e in range(experts_local)], axis=0)
            summed = lax.dot_general(
                picks[group], value, (((0,), (0,)), ((), ())), preferred_element_type=jnp.float32
            )
            out[pl.ds(pl.multiple_of(group * width, width), width), :] = summed.astype(
                jnp.bfloat16
            )


def run_experts(aux, rows, gate_weight, up_weight, down_weight, capacity):
    count, doubled, row_count = aux.shape
    experts_local, depth, hidden = gate_weight.shape
    groups = count // 2
    slots = -(-4 * capacity // 16) * 16
    whole = dict(pipeline_mode=pl.Buffered(1))
    return pl.pallas_call(
        functools.partial(expert_kernel, capacity, slots, doubled // 2),
        grid=(experts_local,),
        out_shape=jax.ShapeDtypeStruct(rows.shape, jnp.bfloat16),
        in_specs=[
            pl.BlockSpec(aux.shape, lambda e: (0, 0, 0), **whole),
            pl.BlockSpec(rows.shape, lambda e: (0, 0), **whole),
            pl.BlockSpec((1, depth, hidden), lambda e: (e, 0, 0)),
            pl.BlockSpec((1, depth, hidden), lambda e: (e, 0, 0)),
            pl.BlockSpec((1, hidden, depth), lambda e: (e, 0, 0)),
        ],
        out_specs=pl.BlockSpec(rows.shape, lambda e: (0, 0), **whole),
        scratch_shapes=[
            pltpu.VMEM((groups, experts_local * slots, 2 * row_count), jnp.bfloat16),
            pltpu.VMEM((experts_local, groups, slots, 1), jnp.float32),
            pltpu.VMEM((experts_local, groups, slots, depth), jnp.bfloat16),
            pltpu.VMEM((experts_local, groups, slots, depth), jnp.bfloat16),
        ],
        compiler_params=pltpu.CompilerParams(
            dimension_semantics=("arbitrary",), vmem_limit_bytes=62 * 2**20
        ),
    )(aux, rows, gate_weight, up_weight, down_weight)


def body(
    queries,
    new_keys,
    new_values,
    cache_keys,
    cache_values,
    cache_lens,
    residual,
    out_weight,
    norm_gain,
    expert_ids,
    route_weights,
    gate_weight,
    up_weight,
    down_weight,
):
    devices = lax.axis_size("tok")
    group = HEADS // KVH
    row_count = residual.shape[0]
    block_rows = row_count // 2
    top_count = expert_ids.shape[1]
    experts_local = gate_weight.shape[0]
    experts_all = experts_local * devices
    capacity = max(2, block_rows * top_count * 3 // (2 * experts_all))
    cache_rows = cache_keys.shape[0]
    length = cache_lens[0]
    key_all = jnp.concatenate([cache_keys, new_keys], 0).reshape(-1, KVH, HD).transpose(1, 0, 2)
    value_all = (
        jnp.concatenate([cache_values, new_values], 0).reshape(-1, KVH, HD).transpose(1, 0, 2)
    )
    place = lax.axis_index("tok")
    core = place % 2
    same_core = [list(range(parity, devices, 2)) for parity in range(2)]
    swap = [(i, i ^ 1) for i in range(devices)]
    groups = lax.axis_size("groups")
    part = lax.axis_index("groups")
    piece_rows = out_weight.shape[0] // groups
    piece = lax.dynamic_slice_in_dim(out_weight, part * piece_rows, piece_rows, 0)
    core_weight = lax.all_gather(
        piece, "tok", axis=0, tiled=True, axis_index_groups=same_core
    )
    positions = jnp.arange(row_count)
    cache_ok = jnp.broadcast_to(jnp.arange(cache_rows)[None, :] < length, (row_count, cache_rows))
    new_ok = jnp.arange(new_keys.shape[0])[None, :] <= positions[:, None]
    allowed = jnp.concatenate([cache_ok, new_ok], 1)
    shaped = queries.reshape(row_count, KVH, group, HD).transpose(1, 0, 2, 3)
    output = head_attention(shaped, key_all, value_all, allowed)
    attended = output.transpose(1, 0, 2, 3).reshape(
        row_count, devices // 2, 2, groups, piece_rows
    )
    own_columns = lax.dynamic_index_in_dim(attended, core, 2, keepdims=False)
    other_columns = lax.dynamic_index_in_dim(attended, 1 - core, 2, keepdims=False)
    sibling_columns = lax.ppermute(other_columns, "tok", swap)
    both = jnp.concatenate([own_columns, sibling_columns], 0)
    projected = []
    for step in range(groups):
        rows = lax.dynamic_index_in_dim(both, (part + step) % groups, 2, keepdims=False)
        rows = rows.reshape(2 * row_count, -1)
        if step:
            ahead = [(i, (i + step) % groups) for i in range(groups)]
            rows = lax.ppermute(rows, "groups", ahead)
        projected.append(jnp.dot(rows, core_weight, preferred_element_type=jnp.float32))
    mixed = residual.astype(jnp.float32)
    for step in reversed(range(groups)):
        from_sibling = lax.ppermute(
            projected[step][row_count:].astype(jnp.bfloat16), "tok", swap
        )
        summed_rows = projected[step][:row_count] + from_sibling.astype(jnp.float32)
        if step:
            back = [(i, (i - step) % groups) for i in range(groups)]
            summed_rows = lax.ppermute(summed_rows.astype(jnp.bfloat16), "groups", back)
        mixed = mixed + summed_rows.astype(jnp.float32)
    factor = lax.rsqrt(jnp.mean(mixed * mixed, axis=-1, keepdims=True) + 1e-06)
    normed = (mixed * factor * norm_gain).astype(jnp.bfloat16)
    aux = jnp.concatenate([expert_ids.astype(jnp.float32).T, route_weights.T], axis=0)
    all_rows, all_aux = gather_rows(normed, aux, devices)
    summed = run_experts(
        all_aux,
        all_rows.reshape(devices * row_count, -1),
        gate_weight,
        up_weight,
        down_weight,
        capacity,
    )
    return sum_rows(summed.reshape(devices, row_count, -1), mixed, devices)


def solution(mesh):
    placed = (
        P(("groups", "tok"), None),
        P(("groups", "tok"), None),
        P(("groups", "tok"), None),
        P(("groups", "tok"), None),
        P(("groups", "tok"), None),
        P(("groups", "tok")),
        P(("groups", "tok"), None),
        P("tok", None),
        P(),
        P(("groups", "tok"), None),
        P(("groups", "tok"), None),
        P("tok", None, None),
        P("tok", None, None),
        P("tok", None, None),
    )
    return jax.shard_map(
        body, mesh=mesh, in_specs=placed, out_specs=P(("groups", "tok"), None), check_vma=False
    )
```
